256 devices in a mesh: ctx: 32 (over z, x), head: 8 (over y, core).
Axes of the slice: x: 4, y: 4, z: 8, core: 2. Of those that a mesh axis runs over, the one named last changes fastest.
Arguments:
- query_rows: bfloat16 [32768, 6144], P(('ctx', 'head')), may hold values from -0.52734375 to 0.52734375
- key_rows: bfloat16 [32768, 6144], P(('ctx', 'head')), may hold values from -0.52734375 to 0.52734375
- value_rows: bfloat16 [32768, 6144], P(('ctx', 'head')), may hold values from -0.4453125 to 0.4453125
- grad_out: bfloat16 [32768, 6144], P(('ctx', 'head')), may hold values from -0.4453125 to 0.4453125
- decay_rates: float32 [48], replicated, as said below
Outputs:
- query_gradient: bfloat16 [32768, 6144], P(('ctx', 'head'))
- grad_key: bfloat16 [32768, 6144], P(('ctx', 'head'))
- value_gradient: bfloat16 [32768, 6144], P(('ctx', 'head'))
The draws below stay inside these ranges and needn't reach their ends.
Inputs may be any that keep to these rules, and one draw needn't show every extreme that they name: decay_rates lie between 0.1 / 32768 and 24 / 256.
All inputs are finite; a program needn't handle non-finite values.
Results may differ from the reference program's by a relative error of at most 0.0056.
Values may be sent and summed in bfloat16 or wider, within the bound.
A program may use at most 128 MiB of HBM per device.

```python
import jax
import jax.numpy as jnp
from jax import lax

HEADS = 48
DH = 128
BLOCK = 256
TOKENS = 32768


def draw_decay_rates(key, part):
    pick_key, slow_key, fast_key = jax.random.split(key, 3)
    order = jax.random.permutation(pick_key, HEADS)
    slow_low = 0.1 / TOKENS
    slow_high = 2.0 / TOKENS
    fast_low = 12.0 / BLOCK
    fast_high = 24.0 / BLOCK
    slow = jnp.exp(jax.random.uniform(slow_key, (HEADS,), jnp.float32, jnp.log(slow_low), jnp.log(slow_high)))
    fast = jnp.exp(jax.random.uniform(fast_key, (HEADS,), jnp.float32, jnp.log(fast_low), jnp.log(fast_high)))
    fast_heads = order < HEADS // 2
    return jnp.where(fast_heads, fast, slow).astype(jnp.float32)


def shard_levels(key, extent, shards, low, top_value):
    loudness, own = 1.0, jax.random.fold_in(key, 6)
    for dim, shards_of in shards:
        heights = jnp.exp(jax.random.uniform(jax.random.fold_in(own, dim), (shards_of,), jnp.float32, low / len(shards), top_value / len(shards)))
        loudness = loudness * jnp.repeat(heights, extent[dim] // shards_of).reshape([-1 if axis == dim else 1 for axis in range(len(extent))])
    return loudness


def gaussian(own_key, shape, width, most, shards=(), kind=jnp.bfloat16):
    loudness = shard_levels(own_key, shape, shards, -0.22, 0.18) if shards else 1.0
    values = jax.random.normal(own_key, shape, jnp.float32) * width * loudness
    return jnp.minimum(jnp.maximum(values, -most), most).astype(kind)


def setup_inputs(seed: int = 0) -> dict:
    splits = jax.random.split(jax.random.key(seed), 6)
    return {
        "query_rows": gaussian(splits[0], (TOKENS, HEADS * DH), (DH ** -0.5), 0.52734375, ((0, 256),)),
        "key_rows": gaussian(splits[1], (TOKENS, HEADS * DH), (DH ** -0.5), 0.52734375, ((0, 256),)),
        "value_rows": gaussian(splits[2], (TOKENS, HEADS * DH), (TOKENS ** -0.25), 0.4453125, ((0, 256),)),
        "grad_out": gaussian(splits[3], (TOKENS, HEADS * DH), (TOKENS ** -0.25), 0.4453125, ((0, 256),)),
        "decay_rates": draw_decay_rates(jax.random.fold_in(splits[5], 71), 0),
    }


def round_keep(values):
    return lax.optimization_barrier(values.astype(jnp.bfloat16)).astype(jnp.float32)


def one_head(query_col, key_col, value_col, grad_col, rate):
    nblocks = TOKENS // BLOCK
    q_blocks = query_col.astype(jnp.float32).reshape(nblocks, BLOCK, DH)
    key_block_list = key_col.astype(jnp.float32).reshape(nblocks, BLOCK, DH)
    v_blocks = value_col.astype(jnp.float32).reshape(nblocks, BLOCK, DH)
    gradient_block_list = grad_col.astype(jnp.float32).reshape(nblocks, BLOCK, DH)
    position = jnp.arange(BLOCK, dtype=jnp.float32)
    offset = position[:, None] - position[None, :]
    decay_mask = jnp.where(offset >= 0.0, jnp.exp(-rate * jnp.maximum(offset, 0.0)), 0.0)
    weight_gradient_set = round_keep(jnp.einsum('nid,njd->nij', gradient_block_list, v_blocks) * decay_mask[None])
    forward_weight_set = round_keep(jnp.einsum('nid,njd->nij', q_blocks, key_block_list) * decay_mask[None])
    keys_decayed = round_keep(key_block_list * jnp.exp(-rate * (BLOCK - 1.0 - position))[None, :, None])
    decayed_query_rows = round_keep(q_blocks * jnp.exp(-rate * position)[None, :, None])
    block_kv = jnp.einsum('njd,nje->nde', keys_decayed, v_blocks)
    query_decay_block = jnp.einsum('ubh,uby->uhy', decayed_query_rows, gradient_block_list)
    span = jnp.exp(-rate * BLOCK)

    def advance(state, term):
        return span * state + term, state

    start = jnp.zeros((DH, DH), jnp.float32)
    _, state_before = lax.scan(advance, start, block_kv)
    _, state_after = lax.scan(advance, start, query_decay_block, reverse=True)
    state_before_bfloat = round_keep(state_before)
    state_after_bfloat = round_keep(state_after)
    leading_part = jnp.exp(-rate * (position + 1.0))[None, :, None]
    trailing_part = jnp.exp(-rate * (BLOCK - position))[None, :, None]
    query_gradient = jnp.einsum('ytb,ybr->ytr', weight_gradient_set, key_block_list) + leading_part * jnp.einsum('kzu,kpu->kzp', gradient_block_list, state_before_bfloat)
    grad_key = jnp.einsum('nij,nid->njd', weight_gradient_set, q_blocks) + trailing_part * jnp.einsum('nje,nde->njd', v_blocks, state_after_bfloat)
    value_gradient = jnp.einsum('lov,lox->lvx', forward_weight_set, gradient_block_list) + trailing_part * jnp.einsum('cxk,ckh->cxh', key_block_list, state_after_bfloat)
    return (query_gradient.reshape(TOKENS, DH).astype(jnp.bfloat16),
            grad_key.reshape(TOKENS, DH).astype(jnp.bfloat16),
            value_gradient.reshape(TOKENS, DH).astype(jnp.bfloat16))


def reference(query_rows, key_rows, value_rows, grad_out, decay_rates):
    def per_head(index):
        first = (index * DH).astype(jnp.int32)
        return one_head(lax.dynamic_slice_in_dim(query_rows, first, DH, 1),
                        lax.dynamic_slice_in_dim(key_rows, first, DH, 1),
                        lax.dynamic_slice_in_dim(value_rows, first, DH, 1),
                        lax.dynamic_slice_in_dim(grad_out, first, DH, 1),
                        decay_rates[index])

    query_gradient, grad_key, value_gradient = lax.map(per_head, jnp.arange(HEADS, dtype=jnp.int32))

    def regroup(stacked):
        return jnp.transpose(stacked, (1, 0, 2)).reshape(TOKENS, HEADS * DH)

    return (regroup(query_gradient), regroup(grad_key), regroup(value_gradient))
```

```python
import jax
import jax.numpy as jnp
from jax import lax
from jax.experimental import pallas as pl
from jax.experimental.pallas import tpu as pltpu
from jax.sharding import PartitionSpec as P

DH = 128
ROWS = 128
LINES = 32
YS = 4
HEADS = 48
H = 2
CHUNKS = HEADS // (8 * H)
STATES = 2 * H
PART = STATES * DH // LINES
MESH = pl.DeviceIdType.MESH
F32 = jnp.float32
BF16 = jnp.bfloat16


def dot(a, b, dims):
    return lax.dot_general(a, b, ((dims[:1], dims[1:]), ((), ())), preferred_element_type=F32)


def row_index():
    return lax.broadcasted_iota(jnp.int32, (ROWS, DH), 0).astype(F32)


def kernel(
    rates, q_hbm, k_hbm, v_hbm, g_hbm, dq_hbm, dk_hbm, dv_hbm,
    q, k, v, g, dq, dk, dv, dq_in, dk_in, dv_in,
    own_local, c_send, c_recv, y_send, y_recv, t_send, t_recv, b_send, b_recv,
    s_send, s_recv, s_own, x_send, x_recv,
    load_sem, store_sem, cs, cr, ys, yr, ts, tr, bs, br, ss, sr, xs, xr,
):
    line, place = lax.axis_index("ctx"), lax.axis_index("head")
    y, core = place // 2, place % 2
    sibling = (line, place + 1 - 2 * core)

    def along_y(other):
        return (line, other * 2 + core)

    def across(other):
        return (other, place)

    ins = ((k_hbm, k), (v_hbm, v), (q_hbm, q), (g_hbm, g))
    outs = ((dq, dq_hbm), (dk, dk_hbm), (dv, dv_hbm))
    width = 8 * H * DH

    def load(c, n):
        cols = pl.ds(c * width, width)
        return pltpu.make_async_copy(ins[n][0].at[:, cols], ins[n][1].at[:, cols], load_sem.at[c, n])

    def store(c, n):
        cols = pl.ds(c * width, width)
        return pltpu.make_async_copy(outs[n][0].at[:, cols], outs[n][1].at[:, cols], store_sem.at[c, n])

    for c in range(CHUNKS):
        for n in range(4):
            load(c, n).start()

    barrier = pltpu.get_barrier_semaphore()
    pl.semaphore_signal(barrier, inc=1, device_id=sibling, device_id_type=MESH)
    for d in range(1, YS):
        pl.semaphore_signal(barrier, inc=1, device_id=along_y((y + d) % YS), device_id_type=MESH)

    def greet(d, carry):
        pl.semaphore_signal(barrier, inc=1, device_id=across((line + d) % LINES), device_id_type=MESH)
        return carry

    lax.fori_loop(1, LINES, greet, 0)

    def head_of(c, which, owner, e):
        return c * 8 * H + which * 4 * H + owner * H + e

    def cols_of(head):
        return pl.ds(pl.multiple_of(head * DH, DH), DH)

    def remote(src, dst, send, recv, device):
        return pltpu.make_async_remote_copy(
            src_ref=src, dst_ref=dst, send_sem=send, recv_sem=recv, device_id=device, device_id_type=MESH
        )

    def wait_bytes(ref, sem):
        pltpu.make_async_copy(ref, ref, sem).wait()

    def local_states(head):
        r = rates[head]
        cols = cols_of(head)
        row = row_index()
        kd = (k[:, cols].astype(F32) * jnp.exp(-r * (ROWS - 1.0 - row))).astype(BF16)
        qd = (q[:, cols].astype(F32) * jnp.exp(-r * row)).astype(BF16)
        return dot(kd, v[:, cols], (0, 0)), dot(qd, g[:, cols], (0, 0))

    def locals_of(c):
        for n in range(4):
            load(c, n).wait()

        def theirs(i, carry):
            owner, e = i // H, i % H
            kv, qd = local_states(head_of(c, 1 - core, owner, e))
            c_send[c, owner, e] = kv.astype(BF16)
            c_send[c, owner, H + e] = qd.astype(BF16)
            return carry

        lax.fori_loop(0, 4 * H, theirs, 0, unroll=4)
        if c == 0:
            pl.semaphore_wait(barrier, 1 + (YS - 1) + (LINES - 1))
        remote(c_send.at[c], c_recv.at[c], cs.at[c], cr.at[c], sibling).start()

        def mine(i, carry):
            owner, e = i // H, i % H
            kv, qd = local_states(head_of(c, core, owner, e))
            own_local[c, owner, e] = kv
            own_local[c, owner, H + e] = qd
            return carry

        lax.fori_loop(0, 4 * H, mine, 0, unroll=4)

    def decay(r, steps):
        return jnp.exp(jnp.full((1, DH), -r * steps, F32))

    def send_y(c):
        wait_bytes(c_recv.at[c], cr.at[c])
        for d in (2, 1, 3, 0):
            owner = (y + d) % YS
            target = y_recv.at[c, y] if d == 0 else y_send.at[c, owner]
            for e in range(H):
                half = decay(rates[head_of(c, core, owner, e)], float(ROWS))
                one = jnp.ones_like(half)
                for way in range(2):
                    s = way * H + e
                    early = core == way
                    a = jnp.where(early, half, one)
                    b = jnp.where(early, one, half)
                    target[s] = (a * own_local[c, owner, s] + b * c_recv[c, owner, s].astype(F32)).astype(BF16)
            if d != 0:
                remote(y_send.at[c, owner], y_recv.at[c, y], ys.at[c], yr.at[c], along_y(owner)).start()

    def horner(c, s, rows, start):
        way, e = s // H, s % H
        a = decay(rates[head_of(c, core, y, e)], 2.0 * ROWS)
        order = range(YS) if way == 0 else range(YS - 1, -1, -1)
        state, states = start, []
        for chip in order:
            states.append((chip, state))
            term = y_recv[c, chip, s, rows].astype(F32)
            state = term if state is None else a * state + term
        return states, state

    def send_lines(c):
        wait_bytes(y_recv.at[c, pl.ds(0, YS - 1)], yr.at[c])
        for s in range(STATES):
            for part in range(2):
                rows = pl.ds(part * 64, 64)
                t_send[c, s, rows] = horner(c, s, rows, None)[1].astype(BF16)
        per = DH // PART

        def rows_of(ref, p):
            return ref.at[c, p // per, pl.ds(pl.multiple_of((p % per) * PART, PART), PART)]

        def go(d, carry):
            p = (line + d) % LINES
            remote(rows_of(t_send, p), t_recv.at[c, line], ts.at[c], tr.at[c], across(p)).start()
            return carry

        lax.fori_loop(1, LINES, go, 0)
        t_recv[c, line] = rows_of(t_send, line)[...]

    def scan_lines(c):
        wait_bytes(t_recv.at[c, pl.ds(0, LINES - 1)], tr.at[c])
        per = DH // PART
        way, e = line // (LINES // 2), (line // per) % H
        a = decay(rates[head_of(c, core, y, e)], 2.0 * ROWS * YS)

        def step(i, state):
            at = jnp.where(way == 0, i, LINES - 1 - i)
            b_send[c, at] = state.astype(BF16)
            return a * state + t_recv[c, at].astype(F32)

        lax.fori_loop(0, LINES, step, jnp.zeros((PART, DH), F32), unroll=8)

        def rows_of(ref, p):
            return ref.at[c, p // per, pl.ds(pl.multiple_of((p % per) * PART, PART), PART)]

        def go(d, carry):
            p = (line + d) % LINES
            remote(b_send.at[c, p], rows_of(b_recv, line), bs.at[c], br.at[c], across(p)).start()
            return carry

        lax.fori_loop(1, LINES, go, 0)
        rows_of(b_recv, line)[...] = b_send[c, line]

    def send_states(c):
        wait_bytes(t_recv.at[c, pl.ds(0, LINES - 1)], br.at[c])
        for s in range(STATES):
            for part in range(2):
                rows = pl.ds(part * 64, 64)
                for chip, state in horner(c, s, rows, b_recv[c, s, rows].astype(F32))[0]:
                    s_send[c, chip, s, rows] = state.astype(BF16)
        for d in (2, 1, 3):
            chip = (y + d) % YS
            remote(s_send.at[c, chip], s_recv.at[c, y], ss.at[c], sr.at[c], along_y(chip)).start()

    def send_sibling(c):
        wait_bytes(s_recv.at[c, pl.ds(0, YS - 1)], sr.at[c])
        near = 1 - core
        for d in range(YS):
            owner = (y + d) % YS
            source = s_send.at[c, y] if d == 0 else s_recv.at[c, owner]
            for e in range(H):
                half = decay(rates[head_of(c, core, owner, e)], float(ROWS))
                s = near * H + e
                state = source[s]
                s_own[c, owner, s] = (half * state.astype(F32) + c_recv[c, owner, s].astype(F32)).astype(BF16)
                x_send[c, owner, s] = state
                s = core * H + e
                state = source[s]
                s_own[c, owner, s] = state
                x_send[c, owner, s] = (half * state.astype(F32) + own_local[c, owner, s]).astype(BF16)
        remote(x_send.at[c], x_recv.at[c], xs.at[c], xr.at[c], sibling).start()

    def inside(first, count):
        def one(head, carry):
            r = rates[head]
            cols = cols_of(head)
            gap = row_index() - lax.broadcasted_iota(jnp.int32, (ROWS, DH), 1).astype(F32)
            mask = jnp.where(gap >= 0.0, jnp.exp(-r * jnp.maximum(gap, 0.0)), 0.0)
            kh, vh, qh, gh = k[:, cols], v[:, cols], q[:, cols], g[:, cols]
            weights = (dot(gh, vh, (1, 1)) * mask).astype(BF16)
            forward = (dot(qh, kh, (1, 1)) * mask).astype(BF16)
            dq_in[:, cols] = dot(weights, kh, (1, 0))
            dk_in[:, cols] = dot(weights, qh, (0, 0))
            dv_in[:, cols] = dot(forward, gh, (0, 0))
            return carry

        lax.fori_loop(first, first + count, one, 0, unroll=2)

    def finish(c, which, states):
        def one(i, carry):
            owner, e = i // H, i % H
            head = head_of(c, which, owner, e)
            r = rates[head]
            cols = cols_of(head)
            row = row_index()
            lead = jnp.exp(-r * (row + 1.0))
            trail = jnp.exp(-r * (ROWS - row))
            before, after = states[c, owner, e], states[c, owner, H + e]
            dq[:, cols] = (dq_in[:, cols] + lead * dot(g[:, cols], before, (1, 1))).astype(BF16)
            dk[:, cols] = (dk_in[:, cols] + trail * dot(v[:, cols], after, (1, 1))).astype(BF16)
            dv[:, cols] = (dv_in[:, cols] + trail * dot(k[:, cols], after, (1, 0))).astype(BF16)
            return carry

        lax.fori_loop(0, 4 * H, one, 0, unroll=2)

    def finish_all(c):
        finish(c, core, s_own)
        wait_bytes(x_recv.at[c], xr.at[c])
        finish(c, 1 - core, x_recv)
        for n in range(3):
            store(c, n).start()

    locals_of(0)
    locals_of(1)
    send_y(0)
    locals_of(2)
    send_y(1)
    inside(0, 8)
    send_y(2)
    inside(8, 8)
    send_lines(0)
    inside(16, 8)
    send_lines(1)
    scan_lines(0)
    inside(24, 8)
    send_lines(2)
    scan_lines(1)
    inside(32, 8)
    send_states(0)
    scan_lines(2)
    inside(40, 8)
    send_states(1)
    send_states(2)
    send_sibling(0)
    finish_all(0)
    send_sibling(1)
    finish_all(1)
    send_sibling(2)
    finish_all(2)

    for c in range(CHUNKS):
        for n in range(3):
            store(c, n).wait()
        wait_bytes(c_send.at[c], cs.at[c])
        wait_bytes(y_send.at[c, pl.ds(0, YS - 1)], ys.at[c])
        wait_bytes(t_recv.at[c, pl.ds(0, LINES - 1)], ts.at[c])
        wait_bytes(b_send.at[c, pl.ds(0, LINES - 1)], bs.at[c])
        wait_bytes(s_send.at[c, pl.ds(0, YS - 1)], ss.at[c])
        wait_bytes(x_send.at[c], xs.at[c])


def local(query_rows, key_rows, value_rows, grad_out, decay_rates):
    whole = (ROWS, HEADS * DH)
    quad = (CHUNKS, YS, STATES, DH, DH)
    sems = pltpu.SemaphoreType.DMA((CHUNKS,))
    anywhere = pl.BlockSpec(memory_space=pl.ANY)
    return pl.pallas_call(
        kernel,
        out_shape=[jax.ShapeDtypeStruct(whole, BF16)] * 3,
        in_specs=[pl.BlockSpec(memory_space=pltpu.SMEM)] + [anywhere] * 4,
        out_specs=[anywhere] * 3,
        scratch_shapes=[pltpu.VMEM(whole, BF16)] * 7
        + [pltpu.VMEM(whole, F32)] * 3
        + [
            pltpu.VMEM(quad, F32),
            pltpu.VMEM(quad, BF16),
            pltpu.VMEM(quad, BF16),
            pltpu.VMEM(quad, BF16),
            pltpu.VMEM(quad, BF16),
            pltpu.VMEM((CHUNKS, STATES, DH, DH), BF16),
            pltpu.VMEM((CHUNKS, LINES, PART, DH), BF16),
            pltpu.VMEM((CHUNKS, LINES, PART, DH), BF16),
            pltpu.VMEM((CHUNKS, STATES, DH, DH), BF16),
            pltpu.VMEM(quad, BF16),
            pltpu.VMEM(quad, BF16),
            pltpu.VMEM(quad, BF16),
            pltpu.VMEM(quad, BF16),
            pltpu.VMEM(quad, BF16),
            pltpu.SemaphoreType.DMA((CHUNKS, 4)),
            pltpu.SemaphoreType.DMA((CHUNKS, 3)),
        ]
        + [sems] * 12,
        compiler_params=pltpu.CompilerParams(
            collective_id=0, has_side_effects=True, vmem_limit_bytes=60 * 1024 * 1024
        ),
        name="decayed_attention_backward",
    )(decay_rates, query_rows, key_rows, value_rows, grad_out)


def solution(mesh):
    rows = P(("ctx", "head"), None)
    return jax.shard_map(
        local,
        mesh=mesh,
        in_specs=(rows, rows, rows, rows, P()),
        out_specs=(rows, rows, rows),
        check_vma=False,
    )
```

```python
import jax
import jax.numpy as jnp
from jax import lax
from jax.experimental import pallas as pl
from jax.experimental.pallas import tpu as pltpu
from jax.sharding import PartitionSpec as P

DH = 128
ROWS = 128
HEADS = 48
XS, YS, ZS = 4, 4, 8
CHIPS = XS * YS
CHUNKS = HEADS // (2 * YS)
SLICE = 2 * DH // XS
MESH = pl.DeviceIdType.MESH
F32 = jnp.float32
BF16 = jnp.bfloat16


def dot(a, b, dims):
    return lax.dot_general(a, b, ((dims[:1], dims[1:]), ((), ())), preferred_element_type=F32)


def row_index():
    return lax.broadcasted_iota(jnp.int32, (ROWS, DH), 0).astype(F32)


def decay(r, steps):
    return jnp.exp(jnp.full((1, DH), -r * steps, F32))


def remote(src, dst, send, recv, device):
    return pltpu.make_async_remote_copy(
        src_ref=src, dst_ref=dst, send_sem=send, recv_sem=recv, device_id=device, device_id_type=MESH
    )


def wait_bytes(ref, sem):
    pltpu.make_async_copy(ref, ref, sem).wait()


def kernel(
    rates, q_hbm, k_hbm, v_hbm, g_hbm, dq, dk, dv,
    q, k, v, g, dq_in, dk_in, dv_in,
    own_local, c_send, c_recv, e_send, e_recv, l_send, l_recv, z_send, z_recv, s_send, s_recv, x_recv,
    load_sem, cs, cr, es, er, ls, lr, zs, zr, ss, sr, xs, xr,
):
    line, place = lax.axis_index("ctx"), lax.axis_index("head")
    z, x = line // XS, line % XS
    y, core = place // 2, place % 2
    chip = x * YS + y
    sibling = (line, place + 1 - 2 * core)
    way = x // 2
    turn = jnp.where(way == 0, z, ZS - 1 - z)

    def in_plane(to_x, to_y):
        return (z * XS + to_x, to_y * 2 + core)

    def along_z(to_z):
        return (to_z * XS + x, place)

    ins = ((k_hbm, k), (v_hbm, v), (q_hbm, q), (g_hbm, g))

    def load(c, n):
        cols = pl.ds(c * 2 * YS * DH, 2 * YS * DH)
        return pltpu.make_async_copy(ins[n][0].at[:, cols], ins[n][1].at[:, cols], load_sem.at[c, n])

    for c in range(CHUNKS):
        for n in range(4):
            load(c, n).start()

    barrier = pltpu.get_barrier_semaphore()
    pl.semaphore_signal(barrier, inc=1, device_id=sibling, device_id_type=MESH)

    def greet_plane(d, carry):
        to = in_plane((x + d // YS) % XS, (y + d % YS) % YS)
        pl.semaphore_signal(barrier, inc=1, device_id=to, device_id_type=MESH)
        return carry

    def greet_z(d, carry):
        pl.semaphore_signal(barrier, inc=1, device_id=along_z((z + d) % ZS), device_id_type=MESH)
        return carry

    lax.fori_loop(1, CHIPS, greet_plane, 0)
    lax.fori_loop(1, ZS, greet_z, 0)

    def head_of(c, which, owner):
        return (c * 2 + which) * YS + owner

    def cols_of(head):
        return pl.ds(pl.multiple_of(head * DH, DH), DH)

    def slice_of(index):
        return pl.ds(pl.multiple_of(index * SLICE, SLICE), SLICE)

    def local_states(head):
        r = rates[head]
        cols = cols_of(head)
        row = row_index()
        kd = (k[:, cols].astype(F32) * jnp.exp(-r * (ROWS - 1.0 - row))).astype(BF16)
        qd = (q[:, cols].astype(F32) * jnp.exp(-r * row)).astype(BF16)
        return dot(kd, v[:, cols], (0, 0)), dot(qd, g[:, cols], (0, 0))

    def locals_of(c):
        for n in range(4):
            load(c, n).wait()

        def theirs(owner, carry):
            kv, qd = local_states(head_of(c, 1 - core, owner))
            c_send[c, 0, owner] = kv.astype(BF16)
            c_send[c, 1, owner] = qd.astype(BF16)
            return carry

        lax.fori_loop(0, YS, theirs, 0, unroll=True)
        if c == 0:
            pl.semaphore_wait(barrier, 1 + (CHIPS - 1) + (ZS - 1))
        remote(c_send.at[c], c_recv.at[c], cs.at[c], cr.at[c], sibling).start()

        def mine(owner, carry):
            kv, qd = local_states(head_of(c, core, owner))
            own_local[c, owner, 0] = kv
            own_local[c, owner, 1] = qd
            e_send[c, owner] = jnp.where(core == 0, kv, qd).astype(BF16)
            return carry

        lax.fori_loop(0, YS, mine, 0, unroll=True)
        remote(e_send.at[c], e_recv.at[c], es.at[c], er.at[c], sibling).start()

    def send_locals(c):
        wait_bytes(c_recv.at[c], cr.at[c])
        for dy in (2, 1, 3, 0):
            to_y = (y + dy) % YS
            half = decay(rates[head_of(c, core, to_y)], float(ROWS))
            one = jnp.ones_like(half)
            for w in range(2):
                a = jnp.where(core == w, half, one)
                b = jnp.where(core == w, one, half)
                both = a * own_local[c, to_y, w] + b * c_recv[c, w, to_y].astype(F32)
                l_send[c, to_y, pl.ds(w * DH, DH)] = both.astype(BF16)
            for dx in (2, 1, 3, 0):
                to_x = (x + dx) % XS
                if dx or dy:
                    remote(
                        l_send.at[c, to_y, slice_of(to_x)], l_recv.at[c, chip], ls.at[c], lr.at[c],
                        in_plane(to_x, to_y),
                    ).start()
                else:
                    l_recv[c, chip] = l_send[c, y, slice_of(x)]

    def send_plane(c):
        wait_bytes(l_recv.at[c, pl.ds(0, CHIPS - 1)], lr.at[c])
        a = decay(rates[head_of(c, core, y)], 2.0 * ROWS)

        def step(i, state):
            return a * state + l_recv[c, jnp.where(way == 0, i, CHIPS - 1 - i)].astype(F32)

        z_send[c] = lax.fori_loop(0, CHIPS, step, jnp.zeros((SLICE, DH), F32), unroll=True)

        def go(i, carry):
            to_z = jnp.where(way == 0, i, ZS - 1 - i)
            remote(z_send.at[c], z_recv.at[c, z], zs.at[c, i], zr.at[c, z], along_z(to_z)).start()
            return carry

        lax.fori_loop(turn + 1, ZS, go, 0)

    def send_states(c):
        r = rates[head_of(c, core, y)]
        a, plane = decay(r, 2.0 * ROWS), decay(r, 2.0 * ROWS * CHIPS)

        def from_planes(i, state):
            at = jnp.where(way == 0, i, ZS - 1 - i)
            wait_bytes(z_recv.at[c, at], zr.at[c, at])
            return plane * state + z_recv[c, at]

        state = lax.fori_loop(0, turn, from_planes, jnp.zeros((SLICE, DH), F32))

        def step(i, state):
            at = jnp.where(way == 0, i, CHIPS - 1 - i)
            s_send[c, at] = state.astype(BF16)
            return a * state + l_recv[c, at].astype(F32)

        lax.fori_loop(0, CHIPS, step, state, unroll=True)
        for dy in (2, 1, 3, 0):
            for dx in (2, 1, 3, 0):
                to_x, to_y = (x + dx) % XS, (y + dy) % YS
                if dx or dy:
                    remote(
                        s_send.at[c, to_x * YS + to_y], s_recv.at[c, y, slice_of(x)], ss.at[c], sr.at[c],
                        in_plane(to_x, to_y),
                    ).start()
        s_recv[c, y, slice_of(x)] = s_send[c, chip]

    def forward(c):
        wait_bytes(l_recv.at[c, pl.ds(0, CHIPS - 1)], sr.at[c])
        remote(s_recv.at[c], x_recv.at[c], xs.at[c], xr.at[c], sibling).start()

    def inside(c, which):
        def one(owner, reads_back):
            head = head_of(c, which, owner)
            r = rates[head]
            cols = cols_of(head)
            row = row_index()
            gap = row - lax.broadcasted_iota(jnp.int32, (ROWS, DH), 1).astype(F32)
            mask = jnp.where(gap >= 0.0, jnp.exp(-r * jnp.maximum(gap, 0.0)), 0.0)
            kh, vh, qh, gh = k[:, cols], v[:, cols], q[:, cols], g[:, cols]
            weights = (dot(gh, vh, (1, 1)) * mask).astype(BF16)
            forwards = (dot(qh, kh, (1, 1)) * mask).astype(BF16)
            grad_q = dot(weights, kh, (1, 0))
            grad_k = dot(weights, qh, (0, 0))
            grad_v = dot(forwards, gh, (0, 0))
            if reads_back:
                before = c_recv[c, 0, owner] if which is core else e_recv[c, owner]
                grad_q += jnp.exp(-r * (row + 1.0)) * dot(gh, before, (1, 1))
            else:
                after = c_recv[c, 1, owner] if which is core else e_recv[c, owner]
                trail = jnp.exp(-r * (ROWS - row))
                grad_k += trail * dot(vh, after, (1, 1))
                grad_v += trail * dot(kh, after, (1, 0))
            dq_in[:, cols] = grad_q
            dk_in[:, cols] = grad_k
            dv_in[:, cols] = grad_v

        for reads_back in (True, False):

            @pl.when(core == int(reads_back))
            def _():
                def body(owner, carry):
                    one(owner, reads_back)
                    return carry

                lax.fori_loop(0, YS, body, 0, unroll=2)

    def inside_own(c):
        inside(c, core)

    def inside_other(c):
        wait_bytes(e_recv.at[c], er.at[c])
        inside(c, 1 - core)

    def finish(c, which, states):
        def one(owner, carry):
            head = head_of(c, which, owner)
            r = rates[head]
            cols = cols_of(head)
            row = row_index() + (core * ROWS).astype(F32)
            lead = jnp.exp(-r * (row + 1.0))
            trail = jnp.exp(-r * (2.0 * ROWS - row))
            before, after = states[c, owner, pl.ds(0, DH)], states[c, owner, pl.ds(DH, DH)]
            dq[:, cols] = (dq_in[:, cols] + lead * dot(g[:, cols], before, (1, 1))).astype(BF16)
            dk[:, cols] = (dk_in[:, cols] + trail * dot(v[:, cols], after, (1, 1))).astype(BF16)
            dv[:, cols] = (dv_in[:, cols] + trail * dot(k[:, cols], after, (1, 0))).astype(BF16)
            return carry

        lax.fori_loop(0, YS, one, 0, unroll=2)

    locals_of(0)
    locals_of(1)
    send_locals(0)
    locals_of(2)
    send_locals(1)
    locals_of(3)
    send_locals(2)
    locals_of(4)
    send_locals(3)
    locals_of(5)
    send_locals(4)
    send_locals(5)
    inside_own(0)
    send_plane(0)
    inside_other(0)
    send_plane(1)
    inside_own(1)
    send_plane(2)
    send_states(0)
    inside_other(1)
    send_plane(3)
    send_states(1)
    inside_own(2)
    send_plane(4)
    send_states(2)
    inside_other(2)
    send_plane(5)
    send_states(3)
    inside_own(3)
    send_states(4)
    inside_other(3)
    inside_own(4)
    send_states(5)
    inside_other(4)
    inside_own(5)
    inside_other(5)
    for c in range(CHUNKS):
        forward(c)
        finish(c, core, s_recv)
        wait_bytes(x_recv.at[c], xr.at[c])
        finish(c, 1 - core, x_recv)

    for c in range(CHUNKS):
        wait_bytes(c_send.at[c], cs.at[c])
        wait_bytes(e_send.at[c], es.at[c])
        wait_bytes(l_recv.at[c, pl.ds(0, CHIPS - 1)], ls.at[c])
        wait_bytes(s_send.at[c, pl.ds(0, CHIPS - 1)], ss.at[c])
        wait_bytes(s_recv.at[c], xs.at[c])

        def sent(i, carry):
            wait_bytes(z_send.at[c], zs.at[c, i])
            return carry

        lax.fori_loop(turn + 1, ZS, sent, 0)


def local(query_rows, key_rows, value_rows, grad_out, decay_rates):
    whole = (ROWS, HEADS * DH)
    sems = pltpu.SemaphoreType.DMA((CHUNKS,))
    anywhere = pl.BlockSpec(memory_space=pl.ANY)
    return pl.pallas_call(
        kernel,
        out_shape=[pltpu.VMEM(whole, BF16)] * 3,
        in_specs=[pl.BlockSpec(memory_space=pltpu.SMEM)] + [anywhere] * 4,
        out_specs=[pl.BlockSpec(memory_space=pltpu.VMEM)] * 3,
        scratch_shapes=[pltpu.VMEM(whole, BF16)] * 4
        + [pltpu.VMEM(whole, F32)] * 3
        + [
            pltpu.VMEM((CHUNKS, YS, 2, DH, DH), F32),
            pltpu.VMEM((CHUNKS, 2, YS, DH, DH), BF16),
            pltpu.VMEM((CHUNKS, 2, YS, DH, DH), BF16),
            pltpu.VMEM((CHUNKS, YS, DH, DH), BF16),
            pltpu.VMEM((CHUNKS, YS, DH, DH), BF16),
            pltpu.VMEM((CHUNKS, YS, 2 * DH, DH), BF16),
            pltpu.VMEM((CHUNKS, CHIPS, SLICE, DH), BF16),
            pltpu.VMEM((CHUNKS, SLICE, DH), F32),
            pltpu.VMEM((CHUNKS, ZS, SLICE, DH), F32),
            pltpu.VMEM((CHUNKS, CHIPS, SLICE, DH), BF16),
            pltpu.VMEM((CHUNKS, YS, 2 * DH, DH), BF16),
            pltpu.VMEM((CHUNKS, YS, 2 * DH, DH), BF16),
            pltpu.SemaphoreType.DMA((CHUNKS, 4)),
        ]
        + [sems] * 6
        + [pltpu.SemaphoreType.DMA((CHUNKS, ZS))] * 2
        + [sems] * 4,
        compiler_params=pltpu.CompilerParams(
            collective_id=0, has_side_effects=True, vmem_limit_bytes=48 * 1024 * 1024
        ),
        name="decayed_attention_backward",
    )(decay_rates, query_rows, key_rows, value_rows, grad_out)


def solution(mesh):
    rows = P(("ctx", "head"), None)
    return jax.shard_map(
        local,
        mesh=mesh,
        in_specs=(rows, rows, rows, rows, P()),
        out_specs=(rows, rows, rows),
        check_vma=False,
    )
```

```python
import jax
import jax.numpy as jnp
from jax import lax
from jax.experimental import pallas as pl
from jax.experimental.pallas import tpu as pltpu
from jax.sharding import PartitionSpec as P

DH = 128
ROWS = 128
HEADS = 48
XS, YS, ZS = 4, 4, 8
CHIPS = XS * YS
SET = YS
CHUNKS = HEADS // (2 * SET)
PART = DH // XS
LAG = 3
PAIRS = 3
LOCAL_UNROLL = 4
PIECES = 1
AHEAD = 5
MESH = pl.DeviceIdType.MESH
F32 = jnp.float32
BF16 = jnp.bfloat16


AWAY = (
    (2, 2), (2, 1), (1, 2), (2, 3), (3, 2), (1, 1), (3, 3), (0, 2), (2, 0), (1, 3), (3, 1), (0, 1), (3, 0), (0, 3), (1, 0),
)


def dot(a, b, dims):
    return lax.dot_general(a, b, ((dims[:1], dims[1:]), ((), ())), preferred_element_type=F32)


def row_index():
    return lax.broadcasted_iota(jnp.int32, (ROWS, DH), 0).astype(F32)


def decay(r, steps):
    return jnp.exp(jnp.full((1, DH), -r * steps, F32))


def remote(src, dst, send, recv, device):
    return pltpu.make_async_remote_copy(
        src_ref=src, dst_ref=dst, send_sem=send, recv_sem=recv, device_id=device, device_id_type=MESH
    )


def wait_bytes(ref, sem):
    pltpu.make_async_copy(ref, ref, sem).wait()


def kernel(
    rates_hbm, q_hbm, k_hbm, v_hbm, g_hbm, dq, dk, dv,
    rates, rate_sem, q, k, v, g, dq_in, dk_in, dv_in,
    own_local, r_send, r_recv, e_send, e_recv, l_send, l_recv, z_send, z_recv, s_send, states,
    load_sem, rs, rr, es, er, ls, lr, zs, zr, ss, sr, xs, xr,
):
    line, place = lax.axis_index("ctx"), lax.axis_index("head")
    z, x = line // XS, line % XS
    y, core = place // 2, place % 2
    chip = x * YS + y
    sibling = (line, place + 1 - 2 * core)

    def in_plane(to):
        return (z * XS + to // YS, (to % YS) * 2 + core)

    def away(dx, dy):
        return (x + jnp.where(core == 0, dx, XS - dx)) % XS, (y + jnp.where(core == 0, dy, YS - dy)) % YS

    def along_z(to_z):
        return (to_z * XS + x, place)

    ins = ((k_hbm, k), (v_hbm, v), (q_hbm, q), (g_hbm, g))

    def load(c, n):
        cols = pl.ds(pl.multiple_of(c * SET * 2 * DH, SET * 2 * DH), SET * 2 * DH)
        return pltpu.make_async_copy(ins[n][0].at[:, cols], ins[n][1].at[:, cols], load_sem.at[c, n])

    def begin(c, carry):
        for n in range(4):
            load(c, n).start()
        return carry

    fetch = pltpu.make_async_copy(rates_hbm, rates, rate_sem)
    fetch.start()
    begin(0, 0)

    barrier = pltpu.get_barrier_semaphore()
    pl.semaphore_signal(barrier, inc=1, device_id=sibling, device_id_type=MESH)

    def greet_plane(d, carry):
        pl.semaphore_signal(barrier, inc=1, device_id=in_plane((chip + d) % CHIPS), device_id_type=MESH)
        return carry

    def greet_z(d, carry):
        pl.semaphore_signal(barrier, inc=1, device_id=along_z((z + d) % ZS), device_id_type=MESH)
        return carry

    lax.fori_loop(1, CHIPS, greet_plane, 0)
    lax.fori_loop(1, ZS, greet_z, 0)
    begin(1, 0)
    fetch.wait()

    def set_of(c, which):
        return (c * 2 + which) * SET

    def cols_of(head):
        return pl.ds(pl.multiple_of(head * DH, DH), DH)

    def local_states(head):
        r = rates[head]
        cols = cols_of(head)
        row = row_index()
        kd = (k[:, cols].astype(F32) * jnp.exp(-r * (ROWS - 1.0 - row))).astype(BF16)
        qd = (q[:, cols].astype(F32) * jnp.exp(-r * row)).astype(BF16)
        return dot(kd, v[:, cols], (0, 0)), dot(qd, g[:, cols], (0, 0))

    def locals_of(c):
        for n in range(4):
            load(c, n).wait()

        @pl.when(c + 2 < CHUNKS)
        def _():
            begin(c + 2, 0)

        def theirs(owner, carry):
            head = set_of(c, 1 - core) + owner
            kv, qd = local_states(head)
            e_send[head] = jnp.where(core == 0, kv, qd).astype(BF16)
            r_send[c, owner] = jnp.where(core == 0, qd, kv).astype(BF16)
            return carry

        lax.fori_loop(0, SET, theirs, 0, unroll=LOCAL_UNROLL)

        @pl.when(c == 0)
        def _():
            pl.semaphore_wait(barrier, 1 + (CHIPS - 1) + (ZS - 1))

        heads = pl.ds(set_of(c, 1 - core), SET)
        remote(e_send.at[heads], e_recv.at[heads], es.at[c, 0], er.at[c, 0], sibling).start()
        remote(r_send.at[c], r_recv.at[c], rs.at[c], rr.at[c], sibling).start()

        def mine(owner, carry):
            head = set_of(c, core) + owner
            kv, qd = local_states(head)
            own_local[c, owner, 0] = kv
            own_local[c, owner, 1] = qd
            e_send[head] = jnp.where(core == 0, kv, qd).astype(BF16)
            return carry

        lax.fori_loop(0, SET, mine, 0, unroll=LOCAL_UNROLL)
        heads = pl.ds(set_of(c, core), SET)
        remote(e_send.at[heads], e_recv.at[heads], es.at[c, 1], er.at[c, 1], sibling).start()

    def send_locals(c):
        wait_bytes(r_recv.at[c], rr.at[c])
        wait_bytes(r_recv.at[c], er.at[c, 0])

        def head_done(i, carry):
            to_y = i
            head = set_of(c, core) + to_y
            half = decay(rates[head], float(ROWS))
            same = own_local[c, to_y, core] * half + r_recv[c, to_y].astype(F32)
            other = own_local[c, to_y, 1 - core] + half * e_recv[head].astype(F32)
            l_send[c, to_y, :, core] = same.astype(BF16).reshape(XS, PART, DH)
            l_send[c, to_y, :, 1 - core] = other.astype(BF16).reshape(XS, PART, DH)

            return carry

        lax.fori_loop(0, YS, head_done, 0)
        for dx, dy in AWAY:
            to_x, to_y = away(dx, dy)
            remote(
                l_send.at[c, to_y, to_x], l_recv.at[c, chip], ls.at[c], lr.at[c], in_plane(to_x * YS + to_y)
            ).start()
        l_recv[c, chip] = l_send[c, y, x]

    def send_plane(c):
        wait_bytes(l_recv.at[c, pl.ds(0, CHIPS - 1)], lr.at[c])
        a = decay(rates[set_of(c, core) + y], 2.0 * ROWS)

        def step(i, both):
            kv, qd = both
            kv = a * kv + l_recv[c, i, 0].astype(F32)
            qd = a * qd + l_recv[c, CHIPS - 1 - i, 1].astype(F32)
            return kv, qd

        zero = jnp.zeros((PART, DH), F32)
        kv, qd = lax.fori_loop(0, CHIPS, step, (zero, zero), unroll=4)
        z_send[c, 0] = kv
        z_send[c, 1] = qd

        def go(d, carry):
            to = (z + d) % ZS
            which = jnp.where(to > z, 0, 1)
            remote(z_send.at[c, which], z_recv.at[c, z], zs.at[c], zr.at[c], along_z(to)).start()
            return carry

        lax.fori_loop(1, ZS, go, 0)

    def send_states(c):
        wait_bytes(z_recv.at[c, pl.ds(0, ZS - 1)], zr.at[c])
        head = set_of(c, core) + y
        a, plane = decay(rates[head], 2.0 * ROWS), decay(rates[head], 2.0 * ROWS * CHIPS)
        zero = jnp.zeros((PART, DH), F32)
        kv = lax.fori_loop(0, z, lambda i, state: plane * state + z_recv[c, i], zero)
        qd = lax.fori_loop(0, ZS - 1 - z, lambda i, state: plane * state + z_recv[c, ZS - 1 - i], zero)

        def step(i, both):
            kv, qd = both
            s_send[c, i, 0] = kv.astype(BF16)
            s_send[c, CHIPS - 1 - i, 1] = qd.astype(BF16)
            kv = a * kv + l_recv[c, i, 0].astype(F32)
            qd = a * qd + l_recv[c, CHIPS - 1 - i, 1].astype(F32)
            return kv, qd

        lax.fori_loop(0, CHIPS, step, (kv, qd), unroll=4)

        for dx, dy in AWAY:
            to_x, to_y = away(dx, dy)
            to = to_x * YS + to_y
            remote(s_send.at[c, to], states.at[head, x], ss.at[c], sr.at[c], in_plane(to)).start()
        states[head, x] = s_send[c, chip]

    def inside(pair, carry):
        def one(head, reads_back):
            r = rates[head]
            cols = cols_of(head)
            row = row_index()
            gap = row - lax.broadcasted_iota(jnp.int32, (ROWS, DH), 1).astype(F32)
            mask = jnp.where(gap >= 0.0, jnp.exp(-r * jnp.maximum(gap, 0.0)), 0.0)
            kh, vh, qh, gh = k[:, cols], v[:, cols], q[:, cols], g[:, cols]
            weights = (dot(gh, vh, (1, 1)) * mask).astype(BF16)
            forwards = (dot(qh, kh, (1, 1)) * mask).astype(BF16)
            grad_q = dot(weights, kh, (1, 0))
            grad_k = dot(weights, qh, (0, 0))
            grad_v = dot(forwards, gh, (0, 0))
            near = e_recv[head]
            if reads_back:
                grad_q += jnp.exp(-r * (row + 1.0)) * dot(gh, near, (1, 1))
            else:
                trail = jnp.exp(-r * (ROWS - row))
                grad_k += trail * dot(vh, near, (1, 1))
                grad_v += trail * dot(kh, near, (1, 0))
            dq_in[:, cols] = grad_q
            dk_in[:, cols] = grad_k
            dv_in[:, cols] = grad_v

        for reads_back in (True, False):

            @pl.when(core == int(reads_back))
            def _():
                one(2 * pair, reads_back)
                one(2 * pair + 1, reads_back)

        return carry

    def finish(first):
        def one(i, carry):
            head = first + i
            r = rates[head]
            cols = cols_of(head)
            row = row_index() + (core * ROWS).astype(F32)
            lead = jnp.exp(-r * (row + 1.0))
            trail = jnp.exp(-r * (2.0 * ROWS - row))
            before = states[head, :, 0].reshape(DH, DH)
            after = states[head, :, 1].reshape(DH, DH)
            dq[:, cols] = (dq_in[:, cols] + lead * dot(g[:, cols], before, (1, 1))).astype(BF16)
            dk[:, cols] = (dk_in[:, cols] + trail * dot(v[:, cols], after, (1, 1))).astype(BF16)
            dv[:, cols] = (dv_in[:, cols] + trail * dot(k[:, cols], after, (1, 0))).astype(BF16)
            return carry

        lax.fori_loop(0, SET, one, 0, unroll=2)

    def first_part(t, carry):
        @pl.when(t < CHUNKS)
        def _():
            locals_of(t)

        @pl.when((t >= 1) & (t <= AHEAD))
        def _():
            send_locals(t - 1)

        return carry

    lax.fori_loop(0, CHUNKS, first_part, 0)

    def arrived(c, carry):
        wait_bytes(r_recv.at[c], er.at[c, 1])
        return carry

    lax.fori_loop(0, CHUNKS, arrived, 0)

    def second_part(t, carry):
        @pl.when(t < CHUNKS)
        def _():
            send_plane(t)

        @pl.when(t + AHEAD < CHUNKS)
        def _():
            send_locals(t + AHEAD)

        @pl.when(t >= LAG)
        def _():
            send_states(t - LAG)

        lax.fori_loop(jnp.minimum(PAIRS * t, HEADS // 2), jnp.minimum(PAIRS * (t + 1), HEADS // 2), inside, 0)
        return carry

    lax.fori_loop(0, CHUNKS + LAG, second_part, 0)

    def third_part(t, carry):
        @pl.when(t >= 1)
        def _():
            wait_bytes(states.at[pl.ds(0, SET)], xr.at[t - 1])
            finish(set_of(t - 1, 1 - core))

        @pl.when(t < CHUNKS)
        def _():
            wait_bytes(l_recv.at[t, pl.ds(0, CHIPS - 1)], sr.at[t])
            heads = pl.ds(set_of(t, core), SET)
            remote(states.at[heads], states.at[heads], xs.at[t], xr.at[t], sibling).start()
            finish(set_of(t, core))

        return carry

    lax.fori_loop(0, CHUNKS + 1, third_part, 0)

    def sent(c, carry):
        wait_bytes(r_send.at[c], rs.at[c])
        wait_bytes(r_send.at[c], es.at[c, 0])
        wait_bytes(r_send.at[c], es.at[c, 1])
        wait_bytes(l_recv.at[c, pl.ds(0, CHIPS - 1)], ls.at[c])
        wait_bytes(s_send.at[c, pl.ds(0, CHIPS - 1)], ss.at[c])
        wait_bytes(states.at[pl.ds(0, SET)], xs.at[c])
        wait_bytes(z_recv.at[c, pl.ds(0, ZS - 1)], zs.at[c])
        return carry

    lax.fori_loop(0, CHUNKS, sent, 0)


def write_out(dq, dk, dv, dq_hbm, dk_hbm, dv_hbm, sems):
    rows = ROWS // PIECES
    copies = [
        pltpu.make_async_copy(here.at[pl.ds(i * rows, rows)], there.at[pl.ds(i * rows, rows)], sems.at[n, i])
        for n, (here, there) in enumerate(((dq, dq_hbm), (dk, dk_hbm), (dv, dv_hbm)))
        for i in range(PIECES)
    ]
    for copy in copies:
        copy.start()
    for copy in copies:
        copy.wait()


def local(query_rows, key_rows, value_rows, grad_out, decay_rates):
    whole = (ROWS, HEADS * DH)
    sems = pltpu.SemaphoreType.DMA((CHUNKS,))
    pair_sems = pltpu.SemaphoreType.DMA((CHUNKS, 2))
    anywhere = pl.BlockSpec(memory_space=pl.ANY)
    grads = pl.pallas_call(
        kernel,
        out_shape=[pltpu.VMEM(whole, BF16)] * 3,
        in_specs=[pl.BlockSpec(memory_space=pltpu.HBM)] + [anywhere] * 4,
        out_specs=[pl.BlockSpec(memory_space=pltpu.VMEM)] * 3,
        scratch_shapes=[pltpu.SMEM((HEADS,), F32), pltpu.SemaphoreType.DMA(())]
        + [pltpu.VMEM(whole, BF16)] * 4
        + [pltpu.VMEM(whole, F32)] * 3
        + [
            pltpu.VMEM((CHUNKS, SET, 2, DH, DH), F32),
            pltpu.VMEM((CHUNKS, SET, DH, DH), BF16),
            pltpu.VMEM((CHUNKS, SET, DH, DH), BF16),
            pltpu.VMEM((HEADS, DH, DH), BF16),
            pltpu.VMEM((HEADS, DH, DH), BF16),
            pltpu.VMEM((CHUNKS, SET, XS, 2, PART, DH), BF16),
            pltpu.VMEM((CHUNKS, CHIPS, 2, PART, DH), BF16),
            pltpu.VMEM((CHUNKS, 2, PART, DH), F32),
            pltpu.VMEM((CHUNKS, ZS, PART, DH), F32),
            pltpu.VMEM((CHUNKS, CHIPS, 2, PART, DH), BF16),
            pltpu.VMEM((HEADS, XS, 2, PART, DH), BF16),
            pltpu.SemaphoreType.DMA((CHUNKS, 4)),
            sems, sems, pair_sems, pair_sems, sems, sems, sems, sems, sems, sems, sems, sems,
        ],
        compiler_params=pltpu.CompilerParams(
            collective_id=0, has_side_effects=True, vmem_limit_bytes=48 * 1024 * 1024
        ),
        name="decayed_attention_backward",
    )(decay_rates, query_rows, key_rows, value_rows, grad_out)
    return pl.pallas_call(
        write_out,
        out_shape=[jax.ShapeDtypeStruct(whole, BF16)] * 3,
        in_specs=[anywhere] * 3,
        out_specs=[anywhere] * 3,
        scratch_shapes=[pltpu.SemaphoreType.DMA((3, PIECES))],
        compiler_params=pltpu.CompilerParams(vmem_limit_bytes=1024 * 1024),
        name="write_gradients",
    )(*grads)


def solution(mesh):
    rows = P(("ctx", "head"), None)
    return jax.shard_map(
        local,
        mesh=mesh,
        in_specs=(rows, rows, rows, rows, P()),
        out_specs=(rows, rows, rows),
        check_vma=False,
    )
```

```python
import jax
import jax.numpy as jnp
from jax import lax
from jax.experimental import pallas as pl
from jax.experimental.pallas import tpu as pltpu
from jax.sharding import PartitionSpec as P

DH = 128
ROWS = 128
HEADS = 48
XS, YS, ZS = 4, 4, 8
CHIPS = XS * YS
SET = YS
CHUNKS = HEADS // (2 * SET)
PART = DH // XS
LAG = 3
PAIRS = 3
LOCAL_UNROLL = 4
PIECES = 1
AHEAD = 6
MESH = pl.DeviceIdType.MESH
F32 = jnp.float32
BF16 = jnp.bfloat16


AWAY = (
    (2, 2), (2, 1), (1, 2), (2, 3), (3, 2), (1, 1), (3, 3), (0, 2), (2, 0), (1, 3), (3, 1), (0, 1), (3, 0), (0, 3), (1, 0),
)


def dot(a, b, dims):
    return lax.dot_general(a, b, ((dims[:1], dims[1:]), ((), ())), preferred_element_type=F32)


def row_index():
    return lax.broadcasted_iota(jnp.int32, (ROWS, DH), 0).astype(F32)


def decay(r, steps):
    return jnp.exp(jnp.full((1, DH), -r * steps, F32))


def remote(src, dst, send, recv, device):
    return pltpu.make_async_remote_copy(
        src_ref=src, dst_ref=dst, send_sem=send, recv_sem=recv, device_id=device, device_id_type=MESH
    )


def wait_bytes(ref, sem):
    pltpu.make_async_copy(ref, ref, sem).wait()


def kernel(
    rates_hbm, q_hbm, k_hbm, v_hbm, g_hbm, dq, dk, dv,
    rates, rate_sem, q, k, v, g, dq_in, dk_in, dv_in,
    own_local, r_send, r_recv, e_send, e_recv, l_send, l_recv, z_send, z_recv, s_send, states,
    load_sem, rs, rr, es, er, ls, lr, zs, zr, ss, sr, xs, xr,
):
    line, place = lax.axis_index("ctx"), lax.axis_index("head")
    z, x = line // XS, line % XS
    y, core = place // 2, place % 2
    chip = x * YS + y
    sibling = (line, place + 1 - 2 * core)

    def in_plane(to_x, to_y):
        return (z * XS + to_x, to_y * 2 + core)

    xs_away = [lax.rem(x + jnp.where(core == 0, d, (XS - d) % XS), XS) for d in range(XS)]
    ys_away = [lax.rem(y + jnp.where(core == 0, d, (YS - d) % YS), YS) for d in range(YS)]
    zs_away = [lax.rem(z + jnp.where(core == 0, d, (ZS - d) % ZS), ZS) for d in range(ZS)]

    def along_z(to_z):
        return (to_z * XS + x, place)

    ins = ((k_hbm, k), (v_hbm, v), (q_hbm, q), (g_hbm, g))

    def load(c, n):
        cols = pl.ds(pl.multiple_of(c * SET * 2 * DH, SET * 2 * DH), SET * 2 * DH)
        return pltpu.make_async_copy(ins[n][0].at[:, cols], ins[n][1].at[:, cols], load_sem.at[c, n])

    def begin(c, carry):
        for n in range(4):
            load(c, n).start()
        return carry

    fetch = pltpu.make_async_copy(rates_hbm, rates, rate_sem)
    fetch.start()
    begin(0, 0)

    barrier = pltpu.get_barrier_semaphore()
    pl.semaphore_signal(barrier, inc=1, device_id=sibling, device_id_type=MESH)

    for dx, dy in AWAY:
        to = in_plane(xs_away[dx], ys_away[dy])
        pl.semaphore_signal(barrier, inc=1, device_id=to, device_id_type=MESH)
    for d in range(1, ZS):
        pl.semaphore_signal(barrier, inc=1, device_id=along_z(zs_away[d]), device_id_type=MESH)
    begin(1, 0)
    fetch.wait()

    def set_of(c, which):
        return (c * 2 + which) * SET

    def cols_of(head):
        return pl.ds(pl.multiple_of(head * DH, DH), DH)

    def local_states(head):
        r = rates[head]
        cols = cols_of(head)
        row = row_index()
        kd = (k[:, cols].astype(F32) * jnp.exp(-r * (ROWS - 1.0 - row))).astype(BF16)
        qd = (q[:, cols].astype(F32) * jnp.exp(-r * row)).astype(BF16)
        return dot(kd, v[:, cols], (0, 0)), dot(qd, g[:, cols], (0, 0))

    def locals_of(c):
        for n in range(4):
            load(c, n).wait()

        @pl.when(c + 2 < CHUNKS)
        def _():
            begin(c + 2, 0)

        def theirs(owner, carry):
            head = set_of(c, 1 - core) + owner
            kv, qd = local_states(head)
            e_send[head] = jnp.where(core == 0, kv, qd).astype(BF16)
            r_send[c, owner] = jnp.where(core == 0, qd, kv).astype(BF16)
            return carry

        lax.fori_loop(0, SET, theirs, 0, unroll=LOCAL_UNROLL)

        @pl.when(c == 0)
        def _():
            pl.semaphore_wait(barrier, 1 + (CHIPS - 1) + (ZS - 1))

        heads = pl.ds(set_of(c, 1 - core), SET)
        remote(e_send.at[heads], e_recv.at[heads], es.at[c, 0], er.at[c, 0], sibling).start()
        remote(r_send.at[c], r_recv.at[c], rs.at[c], rr.at[c], sibling).start()

        def mine(owner, carry):
            head = set_of(c, core) + owner
            kv, qd = local_states(head)
            own_local[c, owner, 0] = kv
            own_local[c, owner, 1] = qd
            e_send[head] = jnp.where(core == 0, kv, qd).astype(BF16)
            return carry

        lax.fori_loop(0, SET, mine, 0, unroll=LOCAL_UNROLL)
        heads = pl.ds(set_of(c, core), SET)
        remote(e_send.at[heads], e_recv.at[heads], es.at[c, 1], er.at[c, 1], sibling).start()

    def send_locals(c):
        wait_bytes(r_recv.at[c], rr.at[c])
        wait_bytes(r_recv.at[c], er.at[c, 0])

        def head_done(i, carry):
            to_y = i
            head = set_of(c, core) + to_y
            half = decay(rates[head], float(ROWS))
            same = own_local[c, to_y, core] * half + r_recv[c, to_y].astype(F32)
            other = own_local[c, to_y, 1 - core] + half * e_recv[head].astype(F32)
            l_send[c, to_y, :, core] = same.astype(BF16).reshape(XS, PART, DH)
            l_send[c, to_y, :, 1 - core] = other.astype(BF16).reshape(XS, PART, DH)

            return carry

        lax.fori_loop(0, YS, head_done, 0, unroll=2)
        for dx, dy in AWAY:
            to_x, to_y = xs_away[dx], ys_away[dy]
            remote(
                l_send.at[c, to_y, to_x], l_recv.at[c, chip], ls.at[c], lr.at[c], in_plane(to_x, to_y)
            ).start()
        l_recv[c, chip] = l_send[c, y, x]

    def send_plane(c):
        wait_bytes(l_recv.at[c, pl.ds(0, CHIPS - 1)], lr.at[c])
        a = decay(rates[set_of(c, core) + y], 2.0 * ROWS)

        def step(i, both):
            kv, qd = both
            kv = a * kv + l_recv[c, i, 0].astype(F32)
            qd = a * qd + l_recv[c, CHIPS - 1 - i, 1].astype(F32)
            return kv, qd

        zero = jnp.zeros((PART, DH), F32)
        kv, qd = lax.fori_loop(0, CHIPS, step, (zero, zero), unroll=True)
        z_send[c, 0] = kv
        z_send[c, 1] = qd

        for d in (4, 3, 5, 2, 6, 1, 7):
            to = zs_away[d]
            which = jnp.where(to > z, 0, 1)
            remote(z_send.at[c, which], z_recv.at[c, z], zs.at[c], zr.at[c], along_z(to)).start()

    def send_states(c):
        wait_bytes(z_recv.at[c, pl.ds(0, ZS - 1)], zr.at[c])
        head = set_of(c, core) + y
        a, plane = decay(rates[head], 2.0 * ROWS), decay(rates[head], 2.0 * ROWS * CHIPS)
        zero = jnp.zeros((PART, DH), F32)
        kv = lax.fori_loop(0, z, lambda i, state: plane * state + z_recv[c, i], zero)
        qd = lax.fori_loop(0, ZS - 1 - z, lambda i, state: plane * state + z_recv[c, ZS - 1 - i], zero)

        def step(i, both):
            kv, qd = both
            s_send[c, i, 0] = kv.astype(BF16)
            s_send[c, CHIPS - 1 - i, 1] = qd.astype(BF16)
            kv = a * kv + l_recv[c, i, 0].astype(F32)
            qd = a * qd + l_recv[c, CHIPS - 1 - i, 1].astype(F32)
            return kv, qd

        lax.fori_loop(0, CHIPS, step, (kv, qd), unroll=True)

        for dx, dy in AWAY:
            to_x, to_y = xs_away[dx], ys_away[dy]
            landing = states.at[head, x]
            remote(s_send.at[c, to_x * YS + to_y], landing, ss.at[c], sr.at[c], in_plane(to_x, to_y)).start()
        states[head, x] = s_send[c, chip]

    def inside(pair, carry):
        def one(head, reads_back):
            r = rates[head]
            cols = cols_of(head)
            row = row_index()
            gap = row - lax.broadcasted_iota(jnp.int32, (ROWS, DH), 1).astype(F32)
            mask = jnp.where(gap >= 0.0, jnp.exp(-r * jnp.maximum(gap, 0.0)), 0.0)
            kh, vh, qh, gh = k[:, cols], v[:, cols], q[:, cols], g[:, cols]
            weights = (dot(gh, vh, (1, 1)) * mask).astype(BF16)
            forwards = (dot(qh, kh, (1, 1)) * mask).astype(BF16)
            grad_q = dot(weights, kh, (1, 0))
            grad_k = dot(weights, qh, (0, 0))
            grad_v = dot(forwards, gh, (0, 0))
            near = e_recv[head]
            if reads_back:
                grad_q += jnp.exp(-r * (row + 1.0)) * dot(gh, near, (1, 1))
            else:
                trail = jnp.exp(-r * (ROWS - row))
                grad_k += trail * dot(vh, near, (1, 1))
                grad_v += trail * dot(kh, near, (1, 0))
            dq_in[:, cols] = grad_q
            dk_in[:, cols] = grad_k
            dv_in[:, cols] = grad_v

        for reads_back in (True, False):

            @pl.when(core == int(reads_back))
            def _():
                one(2 * pair, reads_back)
                one(2 * pair + 1, reads_back)

        return carry

    def finish(first):
        def one(i, carry):
            head = first + i
            r = rates[head]
            cols = cols_of(head)
            row = row_index() + (core * ROWS).astype(F32)
            lead = jnp.exp(-r * (row + 1.0))
            trail = jnp.exp(-r * (2.0 * ROWS - row))
            before = states[head, :, 0].reshape(DH, DH)
            after = states[head, :, 1].reshape(DH, DH)
            dq[:, cols] = (dq_in[:, cols] + lead * dot(g[:, cols], before, (1, 1))).astype(BF16)
            dk[:, cols] = (dk_in[:, cols] + trail * dot(v[:, cols], after, (1, 1))).astype(BF16)
            dv[:, cols] = (dv_in[:, cols] + trail * dot(k[:, cols], after, (1, 0))).astype(BF16)
            return carry

        lax.fori_loop(0, SET, one, 0, unroll=4)

    def first_part(t, carry):
        @pl.when(t < CHUNKS)
        def _():
            locals_of(t)

        @pl.when((t >= 1) & (t <= AHEAD))
        def _():
            send_locals(t - 1)

        return carry

    lax.fori_loop(0, CHUNKS + 1, first_part, 0)

    def arrived(c, carry):
        wait_bytes(r_recv.at[c], er.at[c, 1])
        return carry

    lax.fori_loop(0, CHUNKS, arrived, 0)

    def second_part(t, carry):
        @pl.when(t < CHUNKS)
        def _():
            send_plane(t)

        @pl.when(t >= LAG)
        def _():
            send_states(t - LAG)

        lax.fori_loop(jnp.minimum(PAIRS * t, HEADS // 2), jnp.minimum(PAIRS * (t + 1), HEADS // 2), inside, 0)
        return carry

    lax.fori_loop(0, CHUNKS + LAG, second_part, 0)

    def third_part(t, carry):
        @pl.when(t >= 1)
        def _():
            wait_bytes(states.at[pl.ds(0, SET)], xr.at[t - 1])
            finish(set_of(t - 1, 1 - core))

        @pl.when(t < CHUNKS)
        def _():
            wait_bytes(l_recv.at[t, pl.ds(0, CHIPS - 1)], sr.at[t])
            heads = pl.ds(set_of(t, core), SET)
            remote(states.at[heads], states.at[heads], xs.at[t], xr.at[t], sibling).start()
            finish(set_of(t, core))

        return carry

    lax.fori_loop(0, CHUNKS + 1, third_part, 0)

    def sent(c, carry):
        wait_bytes(r_send.at[c], rs.at[c])
        wait_bytes(r_send.at[c], es.at[c, 0])
        wait_bytes(r_send.at[c], es.at[c, 1])
        wait_bytes(l_recv.at[c, pl.ds(0, CHIPS - 1)], ls.at[c])
        wait_bytes(s_send.at[c, pl.ds(0, CHIPS - 1)], ss.at[c])
        wait_bytes(states.at[pl.ds(0, SET)], xs.at[c])
        wait_bytes(z_recv.at[c, pl.ds(0, ZS - 1)], zs.at[c])
        return carry

    lax.fori_loop(0, CHUNKS, sent, 0)


def write_out(dq, dk, dv, dq_hbm, dk_hbm, dv_hbm, sems):
    rows = ROWS // PIECES
    copies = [
        pltpu.make_async_copy(here.at[pl.ds(i * rows, rows)], there.at[pl.ds(i * rows, rows)], sems.at[n, i])
        for n, (here, there) in enumerate(((dq, dq_hbm), (dk, dk_hbm), (dv, dv_hbm)))
        for i in range(PIECES)
    ]
    for copy in copies:
        copy.start()
    for copy in copies:
        copy.wait()


def local(query_rows, key_rows, value_rows, grad_out, decay_rates):
    whole = (ROWS, HEADS * DH)
    sems = pltpu.SemaphoreType.DMA((CHUNKS,))
    pair_sems = pltpu.SemaphoreType.DMA((CHUNKS, 2))
    anywhere = pl.BlockSpec(memory_space=pl.ANY)
    grads = pl.pallas_call(
        kernel,
        out_shape=[pltpu.VMEM(whole, BF16)] * 3,
        in_specs=[pl.BlockSpec(memory_space=pltpu.HBM)] + [anywhere] * 4,
        out_specs=[pl.BlockSpec(memory_space=pltpu.VMEM)] * 3,
        scratch_shapes=[pltpu.SMEM((HEADS,), F32), pltpu.SemaphoreType.DMA(())]
        + [pltpu.VMEM(whole, BF16)] * 4
        + [pltpu.VMEM(whole, F32)] * 3
        + [
            pltpu.VMEM((CHUNKS, SET, 2, DH, DH), F32),
            pltpu.VMEM((CHUNKS, SET, DH, DH), BF16),
            pltpu.VMEM((CHUNKS, SET, DH, DH), BF16),
            pltpu.VMEM((HEADS, DH, DH), BF16),
            pltpu.VMEM((HEADS, DH, DH), BF16),
            pltpu.VMEM((CHUNKS, SET, XS, 2, PART, DH), BF16),
            pltpu.VMEM((CHUNKS, CHIPS, 2, PART, DH), BF16),
            pltpu.VMEM((CHUNKS, 2, PART, DH), F32),
            pltpu.VMEM((CHUNKS, ZS, PART, DH), F32),
            pltpu.VMEM((CHUNKS, CHIPS, 2, PART, DH), BF16),
            pltpu.VMEM((HEADS, XS, 2, PART, DH), BF16),
            pltpu.SemaphoreType.DMA((CHUNKS, 4)),
            sems, sems, pair_sems, pair_sems, sems, sems, sems, sems, sems, sems, sems, sems,
        ],
        compiler_params=pltpu.CompilerParams(
            collective_id=0, has_side_effects=True, vmem_limit_bytes=57392 * 1024
        ),
        name="decayed_attention_backward",
    )(decay_rates, query_rows, key_rows, value_rows, grad_out)
    return pl.pallas_call(
        write_out,
        out_shape=[jax.ShapeDtypeStruct(whole, BF16)] * 3,
        in_specs=[anywhere] * 3,
        out_specs=[anywhere] * 3,
        scratch_shapes=[pltpu.SemaphoreType.DMA((3, PIECES))],
        compiler_params=pltpu.CompilerParams(vmem_limit_bytes=1024 * 1024),
        name="write_gradients",
    )(*grads)


def solution(mesh):
    rows = P(("ctx", "head"), None)
    return jax.shard_map(
        local,
        mesh=mesh,
        in_specs=(rows, rows, rows, rows, P()),
        out_specs=(rows, rows, rows),
        check_vma=False,
    )
```

```python
import jax
import jax.numpy as jnp
from jax import lax
from jax.experimental import pallas as pl
from jax.experimental.pallas import tpu as pltpu
from jax.sharding import PartitionSpec as P

DH = 128
ROWS = 128
HEADS = 48
XS, YS, ZS = 4, 4, 8
CHIPS = XS * YS
SET = YS
CHUNKS = HEADS // (2 * SET)
PART = DH // XS
LAG = 3
PAIRS = 3
LOCAL_UNROLL = 4
PIECES = 1
AHEAD = 6
MESH = pl.DeviceIdType.MESH
F32 = jnp.float32
BF16 = jnp.bfloat16


AWAY = (
    (2, 2), (2, 1), (1, 2), (2, 3), (3, 2), (1, 1), (3, 3), (0, 2), (2, 0), (1, 3), (3, 1), (0, 1), (3, 0), (0, 3), (1, 0),
)


def dot(a, b, dims):
    return lax.dot_general(a, b, ((dims[:1], dims[1:]), ((), ())), preferred_element_type=F32)


def row_index():
    return lax.broadcasted_iota(jnp.int32, (ROWS, DH), 0).astype(F32)


def decay(r, steps):
    return jnp.exp(jnp.full((1, DH), -r * steps, F32))


def remote(src, dst, send, recv, device):
    return pltpu.make_async_remote_copy(
        src_ref=src, dst_ref=dst, send_sem=send, recv_sem=recv, device_id=device, device_id_type=MESH
    )


def wait_bytes(ref, sem):
    pltpu.make_async_copy(ref, ref, sem).wait()


def kernel(
    rates_hbm, q_hbm, k_hbm, v_hbm, g_hbm, dq, dk, dv,
    rates, rate_sem, q, k, v, g, dq_in, dk_in, dv_in,
    own_local, r_send, r_recv, e_send, e_recv, l_send, l_recv, z_send, z_recv, s_send, states,
    load_sem, rs, rr, es, er, ls, lr, zs, zr, ss, sr, xs, xr,
):
    line, place = lax.axis_index("ctx"), lax.axis_index("head")
    z, x = line // XS, line % XS
    y, core = place // 2, place % 2
    chip = x * YS + y
    sibling = (line, place + 1 - 2 * core)

    def in_plane(to_x, to_y):
        return (z * XS + to_x, to_y * 2 + core)

    xs_away = [lax.rem(x + jnp.where(core == 0, d, (XS - d) % XS), XS) for d in range(XS)]
    ys_away = [lax.rem(y + jnp.where(core == 0, d, (YS - d) % YS), YS) for d in range(YS)]
    zs_away = [lax.rem(z + jnp.where(core == 0, d, (ZS - d) % ZS), ZS) for d in range(ZS)]

    def along_z(to_z):
        return (to_z * XS + x, place)

    ins = ((k_hbm, k), (v_hbm, v), (q_hbm, q), (g_hbm, g))

    def load(c, n):
        cols = pl.ds(pl.multiple_of(c * SET * 2 * DH, SET * 2 * DH), SET * 2 * DH)
        return pltpu.make_async_copy(ins[n][0].at[:, cols], ins[n][1].at[:, cols], load_sem.at[c, n])

    def begin(c, carry):
        for n in range(4):
            load(c, n).start()
        return carry

    fetch = pltpu.make_async_copy(rates_hbm, rates, rate_sem)
    fetch.start()
    begin(0, 0)

    barrier = pltpu.get_barrier_semaphore()
    pl.semaphore_signal(barrier, inc=1, device_id=sibling, device_id_type=MESH)

    for dx, dy in AWAY:
        to = in_plane(xs_away[dx], ys_away[dy])
        pl.semaphore_signal(barrier, inc=1, device_id=to, device_id_type=MESH)
    for d in range(1, ZS):
        pl.semaphore_signal(barrier, inc=1, device_id=along_z(zs_away[d]), device_id_type=MESH)
    begin(1, 0)
    fetch.wait()

    def set_of(c, which):
        return (c * 2 + which) * SET

    def cols_of(head):
        return pl.ds(pl.multiple_of(head * DH, DH), DH)

    def local_states(head):
        r = rates[head]
        cols = cols_of(head)
        row = row_index()
        kd = (k[:, cols].astype(F32) * jnp.exp(-r * (ROWS - 1.0 - row))).astype(BF16)
        qd = (q[:, cols].astype(F32) * jnp.exp(-r * row)).astype(BF16)
        return dot(kd, v[:, cols], (0, 0)), dot(qd, g[:, cols], (0, 0))

    def locals_of(c):
        for n in range(4):
            load(c, n).wait()

        @pl.when(c + 2 < CHUNKS)
        def _():
            begin(c + 2, 0)

        def theirs(owner, carry):
            head = set_of(c, 1 - core) + owner
            kv, qd = local_states(head)
            e_send[head] = jnp.where(core == 0, kv, qd).astype(BF16)
            r_send[c, owner] = jnp.where(core == 0, qd, kv).astype(BF16)
            return carry

        lax.fori_loop(0, SET, theirs, 0, unroll=LOCAL_UNROLL)

        @pl.when(c == 0)
        def _():
            pl.semaphore_wait(barrier, 1 + (CHIPS - 1) + (ZS - 1))

        heads = pl.ds(set_of(c, 1 - core), SET)
        remote(e_send.at[heads], e_recv.at[heads], es.at[c, 0], er.at[c, 0], sibling).start()
        remote(r_send.at[c], r_recv.at[c], rs.at[c], rr.at[c], sibling).start()

        def mine(owner, carry):
            head = set_of(c, core) + owner
            kv, qd = local_states(head)
            own_local[c, owner, 0] = kv
            own_local[c, owner, 1] = qd
            e_send[head] = jnp.where(core == 0, kv, qd).astype(BF16)
            return carry

        lax.fori_loop(0, SET, mine, 0, unroll=LOCAL_UNROLL)
        heads = pl.ds(set_of(c, core), SET)
        remote(e_send.at[heads], e_recv.at[heads], es.at[c, 1], er.at[c, 1], sibling).start()

    def send_locals(c):
        wait_bytes(r_recv.at[c], rr.at[c])
        wait_bytes(r_recv.at[c], er.at[c, 0])

        def head_done(to_y):
            head = set_of(c, core) + to_y
            half = decay(rates[head], float(ROWS))
            same = own_local[c, to_y, core] * half + r_recv[c, to_y].astype(F32)
            other = own_local[c, to_y, 1 - core] + half * e_recv[head].astype(F32)
            l_send[c, to_y, :, core] = same.astype(BF16).reshape(XS, PART, DH)
            l_send[c, to_y, :, 1 - core] = other.astype(BF16).reshape(XS, PART, DH)


        for dy, steps in ((2, (2, 1, 3, 0)), (1, (2, 3, 1, 0)), (3, (2, 1, 3, 0)), (0, (2, 1, 3))):
            to_y = ys_away[dy]
            head_done(to_y)
            for dx in steps:
                to_x = xs_away[dx]
                remote(
                    l_send.at[c, to_y, to_x], l_recv.at[c, chip], ls.at[c], lr.at[c], in_plane(to_x, to_y)
                ).start()
        l_recv[c, chip] = l_send[c, y, x]

    def send_plane(c):
        wait_bytes(l_recv.at[c, pl.ds(0, CHIPS - 1)], lr.at[c])
        a = decay(rates[set_of(c, core) + y], 2.0 * ROWS)

        def step(i, both):
            kv, qd = both
            kv = a * kv + l_recv[c, i, 0].astype(F32)
            qd = a * qd + l_recv[c, CHIPS - 1 - i, 1].astype(F32)
            return kv, qd

        zero = jnp.zeros((PART, DH), F32)
        kv, qd = lax.fori_loop(0, CHIPS, step, (zero, zero), unroll=True)
        z_send[c, 0] = kv
        z_send[c, 1] = qd

        for d in (4, 3, 5, 2, 6, 1, 7):
            to = zs_away[d]
            which = jnp.where(to > z, 0, 1)
            remote(z_send.at[c, which], z_recv.at[c, z], zs.at[c], zr.at[c], along_z(to)).start()

    def send_states(c):
        wait_bytes(z_recv.at[c, pl.ds(0, ZS - 1)], zr.at[c])
        head = set_of(c, core) + y
        a, plane = decay(rates[head], 2.0 * ROWS), decay(rates[head], 2.0 * ROWS * CHIPS)
        zero = jnp.zeros((PART, DH), F32)
        kv = lax.fori_loop(0, z, lambda i, state: plane * state + z_recv[c, i], zero)
        qd = lax.fori_loop(0, ZS - 1 - z, lambda i, state: plane * state + z_recv[c, ZS - 1 - i], zero)

        def step(i, both):
            kv, qd = both
            s_send[c, i, 0] = kv.astype(BF16)
            s_send[c, CHIPS - 1 - i, 1] = qd.astype(BF16)
            kv = a * kv + l_recv[c, i, 0].astype(F32)
            qd = a * qd + l_recv[c, CHIPS - 1 - i, 1].astype(F32)
            return kv, qd

        lax.fori_loop(0, CHIPS, step, (kv, qd), unroll=True)

        for dx, dy in AWAY:
            to_x, to_y = xs_away[dx], ys_away[dy]
            landing = states.at[head, x]
            remote(s_send.at[c, to_x * YS + to_y], landing, ss.at[c], sr.at[c], in_plane(to_x, to_y)).start()
        states[head, x] = s_send[c, chip]

    def inside(pair, carry):
        def one(head, reads_back):
            r = rates[head]
            cols = cols_of(head)
            row = row_index()
            gap = row - lax.broadcasted_iota(jnp.int32, (ROWS, DH), 1).astype(F32)
            mask = jnp.where(gap >= 0.0, jnp.exp(-r * jnp.maximum(gap, 0.0)), 0.0)
            kh, vh, qh, gh = k[:, cols], v[:, cols], q[:, cols], g[:, cols]
            weights = (dot(gh, vh, (1, 1)) * mask).astype(BF16)
            forwards = (dot(qh, kh, (1, 1)) * mask).astype(BF16)
            grad_q = dot(weights, kh, (1, 0))
            grad_k = dot(weights, qh, (0, 0))
            grad_v = dot(forwards, gh, (0, 0))
            near = e_recv[head]
            if reads_back:
                grad_q += jnp.exp(-r * (row + 1.0)) * dot(gh, near, (1, 1))
            else:
                trail = jnp.exp(-r * (ROWS - row))
                grad_k += trail * dot(vh, near, (1, 1))
                grad_v += trail * dot(kh, near, (1, 0))
            dq_in[:, cols] = grad_q
            dk_in[:, cols] = grad_k
            dv_in[:, cols] = grad_v

        for reads_back in (True, False):

            @pl.when(core == int(reads_back))
            def _():
                one(2 * pair, reads_back)
                one(2 * pair + 1, reads_back)

        return carry

    def finish(first):
        def one(i, carry):
            head = first + i
            r = rates[head]
            cols = cols_of(head)
            row = row_index() + (core * ROWS).astype(F32)
            lead = jnp.exp(-r * (row + 1.0))
            trail = jnp.exp(-r * (2.0 * ROWS - row))
            before = states[head, :, 0].reshape(DH, DH)
            after = states[head, :, 1].reshape(DH, DH)
            dq[:, cols] = (dq_in[:, cols] + lead * dot(g[:, cols], before, (1, 1))).astype(BF16)
            dk[:, cols] = (dk_in[:, cols] + trail * dot(v[:, cols], after, (1, 1))).astype(BF16)
            dv[:, cols] = (dv_in[:, cols] + trail * dot(k[:, cols], after, (1, 0))).astype(BF16)
            return carry

        lax.fori_loop(0, SET, one, 0, unroll=4)

    def first_part(t, carry):
        @pl.when(t < CHUNKS)
        def _():
            locals_of(t)

        @pl.when((t >= 1) & (t <= AHEAD))
        def _():
            send_locals(t - 1)

        return carry

    lax.fori_loop(0, CHUNKS + 1, first_part, 0)

    def arrived(c, carry):
        wait_bytes(r_recv.at[c], er.at[c, 1])
        return carry

    lax.fori_loop(0, CHUNKS, arrived, 0)

    def second_part(t, carry):
        @pl.when(t < CHUNKS)
        def _():
            send_plane(t)

        @pl.when(t >= LAG)
        def _():
            send_states(t - LAG)

        lax.fori_loop(jnp.minimum(PAIRS * t, HEADS // 2), jnp.minimum(PAIRS * (t + 1), HEADS // 2), inside, 0)
        return carry

    lax.fori_loop(0, CHUNKS + LAG, second_part, 0)

    def third_part(t, carry):
        @pl.when(t >= 1)
        def _():
            wait_bytes(states.at[pl.ds(0, SET)], xr.at[t - 1])
            finish(set_of(t - 1, 1 - core))

        @pl.when(t < CHUNKS)
        def _():
            wait_bytes(l_recv.at[t, pl.ds(0, CHIPS - 1)], sr.at[t])
            heads = pl.ds(set_of(t, core), SET)
            remote(states.at[heads], states.at[heads], xs.at[t], xr.at[t], sibling).start()
            finish(set_of(t, core))

        return carry

    lax.fori_loop(0, CHUNKS + 1, third_part, 0)

    def sent(c, carry):
        wait_bytes(r_send.at[c], rs.at[c])
        wait_bytes(r_send.at[c], es.at[c, 0])
        wait_bytes(r_send.at[c], es.at[c, 1])
        wait_bytes(l_recv.at[c, pl.ds(0, CHIPS - 1)], ls.at[c])
        wait_bytes(s_send.at[c, pl.ds(0, CHIPS - 1)], ss.at[c])
        wait_bytes(states.at[pl.ds(0, SET)], xs.at[c])
        wait_bytes(z_recv.at[c, pl.ds(0, ZS - 1)], zs.at[c])
        return carry

    lax.fori_loop(0, CHUNKS, sent, 0)


def write_out(dq, dk, dv, dq_hbm, dk_hbm, dv_hbm, sems):
    rows = ROWS // PIECES
    copies = [
        pltpu.make_async_copy(here.at[pl.ds(i * rows, rows)], there.at[pl.ds(i * rows, rows)], sems.at[n, i])
        for n, (here, there) in enumerate(((dq, dq_hbm), (dk, dk_hbm), (dv, dv_hbm)))
        for i in range(PIECES)
    ]
    for copy in copies:
        copy.start()
    for copy in copies:
        copy.wait()


def local(query_rows, key_rows, value_rows, grad_out, decay_rates):
    whole = (ROWS, HEADS * DH)
    sems = pltpu.SemaphoreType.DMA((CHUNKS,))
    pair_sems = pltpu.SemaphoreType.DMA((CHUNKS, 2))
    anywhere = pl.BlockSpec(memory_space=pl.ANY)
    grads = pl.pallas_call(
        kernel,
        out_shape=[pltpu.VMEM(whole, BF16)] * 3,
        in_specs=[pl.BlockSpec(memory_space=pltpu.HBM)] + [anywhere] * 4,
        out_specs=[pl.BlockSpec(memory_space=pltpu.VMEM)] * 3,
        scratch_shapes=[pltpu.SMEM((HEADS,), F32), pltpu.SemaphoreType.DMA(())]
        + [pltpu.VMEM(whole, BF16)] * 4
        + [pltpu.VMEM(whole, F32)] * 3
        + [
            pltpu.VMEM((CHUNKS, SET, 2, DH, DH), F32),
            pltpu.VMEM((CHUNKS, SET, DH, DH), BF16),
            pltpu.VMEM((CHUNKS, SET, DH, DH), BF16),
            pltpu.VMEM((HEADS, DH, DH), BF16),
            pltpu.VMEM((HEADS, DH, DH), BF16),
            pltpu.VMEM((CHUNKS, SET, XS, 2, PART, DH), BF16),
            pltpu.VMEM((CHUNKS, CHIPS, 2, PART, DH), BF16),
            pltpu.VMEM((CHUNKS, 2, PART, DH), F32),
            pltpu.VMEM((CHUNKS, ZS, PART, DH), F32),
            pltpu.VMEM((CHUNKS, CHIPS, 2, PART, DH), BF16),
            pltpu.VMEM((HEADS, XS, 2, PART, DH), BF16),
            pltpu.SemaphoreType.DMA((CHUNKS, 4)),
            sems, sems, pair_sems, pair_sems, sems, sems, sems, sems, sems, sems, sems, sems,
        ],
        compiler_params=pltpu.CompilerParams(
            collective_id=0, has_side_effects=True, vmem_limit_bytes=57392 * 1024
        ),
        name="decayed_attention_backward",
    )(decay_rates, query_rows, key_rows, value_rows, grad_out)
    return pl.pallas_call(
        write_out,
        out_shape=[jax.ShapeDtypeStruct(whole, BF16)] * 3,
        in_specs=[anywhere] * 3,
        out_specs=[anywhere] * 3,
        scratch_shapes=[pltpu.SemaphoreType.DMA((3, PIECES))],
        compiler_params=pltpu.CompilerParams(vmem_limit_bytes=1024 * 1024),
        name="write_gradients",
    )(*grads)


def solution(mesh):
    rows = P(("ctx", "head"), None)
    return jax.shard_map(
        local,
        mesh=mesh,
        in_specs=(rows, rows, rows, rows, P()),
        out_specs=(rows, rows, rows),
        check_vma=False,
    )
```

```python
import jax
import jax.numpy as jnp
from jax import lax
from jax.experimental import pallas as pl
from jax.experimental.pallas import tpu as pltpu
from jax.sharding import PartitionSpec as P

DH = 128
ROWS = 128
HEADS = 48
XS, YS, ZS = 4, 4, 8
CHIPS = XS * YS
SET = YS
CHUNKS = HEADS // (2 * SET)
PART = DH // XS
LAG = 3
PAIRS = 3
LOCAL_UNROLL = 4
PIECES = 1
AHEAD = 6
MESH = pl.DeviceIdType.MESH
F32 = jnp.float32
BF16 = jnp.bfloat16


AWAY = (
    (2, 2), (2, 1), (1, 2), (2, 3), (3, 2), (1, 1), (3, 3), (0, 2), (2, 0), (1, 3), (3, 1), (0, 1), (3, 0), (0, 3), (1, 0),
)


def dot(a, b, dims):
    return lax.dot_general(a, b, ((dims[:1], dims[1:]), ((), ())), preferred_element_type=F32)


def row_index():
    return lax.broadcasted_iota(jnp.int32, (ROWS, DH), 0).astype(F32)


def decay(r, steps):
    return jnp.exp(jnp.full((1, DH), -r * steps, F32))


def remote(src, dst, send, recv, device):
    return pltpu.make_async_remote_copy(
        src_ref=src, dst_ref=dst, send_sem=send, recv_sem=recv, device_id=device, device_id_type=MESH
    )


def wait_bytes(ref, sem):
    pltpu.make_async_copy(ref, ref, sem).wait()


def kernel(
    rates_hbm, q_hbm, k_hbm, v_hbm, g_hbm, dq, dk, dv,
    rates, rate_sem, q, k, v, g, dq_in, dk_in, dv_in,
    own_local, r_send, r_recv, e_send, e_recv, l_send, l_recv, z_send, z_recv, s_send, states,
    load_sem, rs, rr, es, er, ls, lr, zs, zr, ss, sr, xs, xr,
):
    line, place = lax.axis_index("ctx"), lax.axis_index("head")
    z, x = line // XS, line % XS
    y, core = place // 2, place % 2
    chip = x * YS + y
    sibling = (line, place + 1 - 2 * core)

    def in_plane(to_x, to_y):
        return (z * XS + to_x, to_y * 2 + core)

    xs_away = [lax.rem(x + jnp.where(core == 0, d, (XS - d) % XS), XS) for d in range(XS)]
    ys_away = [lax.rem(y + jnp.where(core == 0, d, (YS - d) % YS), YS) for d in range(YS)]
    zs_away = [lax.rem(z + jnp.where(core == 0, d, (ZS - d) % ZS), ZS) for d in range(ZS)]

    def along_z(to_z):
        return (to_z * XS + x, place)

    ins = ((k_hbm, k), (v_hbm, v), (q_hbm, q), (g_hbm, g))

    def load(c, n):
        cols = pl.ds(pl.multiple_of(c * SET * 2 * DH, SET * 2 * DH), SET * 2 * DH)
        return pltpu.make_async_copy(ins[n][0].at[:, cols], ins[n][1].at[:, cols], load_sem.at[c, n])

    def begin(c, carry):
        for n in range(4):
            load(c, n).start()
        return carry

    fetch = pltpu.make_async_copy(rates_hbm, rates, rate_sem)
    fetch.start()
    begin(0, 0)

    barrier = pltpu.get_barrier_semaphore()
    pl.semaphore_signal(barrier, inc=1, device_id=sibling, device_id_type=MESH)

    for dx, dy in AWAY:
        to = in_plane(xs_away[dx], ys_away[dy])
        pl.semaphore_signal(barrier, inc=1, device_id=to, device_id_type=MESH)
    for d in range(1, ZS):
        pl.semaphore_signal(barrier, inc=1, device_id=along_z(zs_away[d]), device_id_type=MESH)
    begin(1, 0)
    fetch.wait()

    def set_of(c, which):
        return (c * 2 + which) * SET

    def cols_of(head):
        return pl.ds(pl.multiple_of(head * DH, DH), DH)

    def local_states(head):
        r = rates[head]
        cols = cols_of(head)
        row = row_index()
        kd = (k[:, cols].astype(F32) * jnp.exp(-r * (ROWS - 1.0 - row))).astype(BF16)
        qd = (q[:, cols].astype(F32) * jnp.exp(-r * row)).astype(BF16)
        return dot(kd, v[:, cols], (0, 0)), dot(qd, g[:, cols], (0, 0))

    def locals_of(c):
        for n in range(4):
            load(c, n).wait()

        @pl.when(c + 2 < CHUNKS)
        def _():
            begin(c + 2, 0)

        def theirs(owner, carry):
            head = set_of(c, 1 - core) + owner
            kv, qd = local_states(head)
            e_send[head] = jnp.where(core == 0, kv, qd).astype(BF16)
            r_send[c, owner] = jnp.where(core == 0, qd, kv).astype(BF16)
            return carry

        lax.fori_loop(0, SET, theirs, 0, unroll=LOCAL_UNROLL)

        @pl.when(c == 0)
        def _():
            pl.semaphore_wait(barrier, 1 + (CHIPS - 1) + (ZS - 1))

        heads = pl.ds(set_of(c, 1 - core), SET)
        remote(e_send.at[heads], e_recv.at[heads], es.at[c, 0], er.at[c, 0], sibling).start()
        remote(r_send.at[c], r_recv.at[c], rs.at[c], rr.at[c], sibling).start()

        def mine(owner, carry):
            head = set_of(c, core) + owner
            kv, qd = local_states(head)
            own_local[c, owner, 0] = kv
            own_local[c, owner, 1] = qd
            e_send[head] = jnp.where(core == 0, kv, qd).astype(BF16)
            return carry

        lax.fori_loop(0, SET, mine, 0, unroll=LOCAL_UNROLL)
        heads = pl.ds(set_of(c, core), SET)
        remote(e_send.at[heads], e_recv.at[heads], es.at[c, 1], er.at[c, 1], sibling).start()

    def send_locals(c):
        wait_bytes(r_recv.at[c], rr.at[c])
        wait_bytes(r_recv.at[c], er.at[c, 0])

        def head_done(i, carry):
            to_y = i
            head = set_of(c, core) + to_y
            half = decay(rates[head], float(ROWS))
            same = own_local[c, to_y, core] * half + r_recv[c, to_y].astype(F32)
            other = own_local[c, to_y, 1 - core] + half * e_recv[head].astype(F32)
            l_send[c, to_y, :, core] = same.astype(BF16).reshape(XS, PART, DH)
            l_send[c, to_y, :, 1 - core] = other.astype(BF16).reshape(XS, PART, DH)

            return carry

        lax.fori_loop(0, YS, head_done, 0, unroll=2)
        for dx, dy in AWAY:
            to_x, to_y = xs_away[dx], ys_away[dy]
            remote(
                l_send.at[c, to_y, to_x], l_recv.at[c, chip], ls.at[c], lr.at[c], in_plane(to_x, to_y)
            ).start()
        l_recv[c, chip] = l_send[c, y, x]

    def send_plane(c):
        wait_bytes(l_recv.at[c, pl.ds(0, CHIPS - 1)], lr.at[c])
        a = decay(rates[set_of(c, core) + y], 2.0 * ROWS)

        def step(i, both):
            kv, qd = both
            kv = a * kv + l_recv[c, i, 0].astype(F32)
            qd = a * qd + l_recv[c, CHIPS - 1 - i, 1].astype(F32)
            return kv, qd

        zero = jnp.zeros((PART, DH), F32)
        kv, qd = lax.fori_loop(0, CHIPS, step, (zero, zero), unroll=True)
        z_send[c, 0] = kv
        z_send[c, 1] = qd

        for d in (4, 3, 5, 2, 6, 1, 7):
            to = zs_away[d]
            which = jnp.where(to > z, 0, 1)
            remote(z_send.at[c, which], z_recv.at[c, z], zs.at[c], zr.at[c], along_z(to)).start()

    def send_states(c):
        wait_bytes(z_recv.at[c, pl.ds(0, ZS - 1)], zr.at[c])
        head = set_of(c, core) + y
        a, plane = decay(rates[head], 2.0 * ROWS), decay(rates[head], 2.0 * ROWS * CHIPS)
        zero = jnp.zeros((PART, DH), F32)
        kv = lax.fori_loop(0, z, lambda i, state: plane * state + z_recv[c, i], zero)
        qd = lax.fori_loop(0, ZS - 1 - z, lambda i, state: plane * state + z_recv[c, ZS - 1 - i], zero)

        def step(i, both):
            kv, qd = both
            s_send[c, i, 0] = kv.astype(BF16)
            s_send[c, CHIPS - 1 - i, 1] = qd.astype(BF16)
            kv = a * kv + l_recv[c, i, 0].astype(F32)
            qd = a * qd + l_recv[c, CHIPS - 1 - i, 1].astype(F32)
            return kv, qd

        lax.fori_loop(0, CHIPS, step, (kv, qd), unroll=True)

        for dx, dy in AWAY:
            to_x, to_y = xs_away[dx], ys_away[dy]
            landing = states.at[head, x]
            remote(s_send.at[c, to_x * YS + to_y], landing, ss.at[c], sr.at[c, y], in_plane(to_x, to_y)).start()
        states[head, x] = s_send[c, chip]

    def inside(pair, carry):
        def one(head, reads_back):
            r = rates[head]
            cols = cols_of(head)
            row = row_index()
            gap = row - lax.broadcasted_iota(jnp.int32, (ROWS, DH), 1).astype(F32)
            mask = jnp.where(gap >= 0.0, jnp.exp(-r * jnp.maximum(gap, 0.0)), 0.0)
            kh, vh, qh, gh = k[:, cols], v[:, cols], q[:, cols], g[:, cols]
            weights = (dot(gh, vh, (1, 1)) * mask).astype(BF16)
            forwards = (dot(qh, kh, (1, 1)) * mask).astype(BF16)
            grad_q = dot(weights, kh, (1, 0))
            grad_k = dot(weights, qh, (0, 0))
            grad_v = dot(forwards, gh, (0, 0))
            near = e_recv[head]
            if reads_back:
                grad_q += jnp.exp(-r * (row + 1.0)) * dot(gh, near, (1, 1))
            else:
                trail = jnp.exp(-r * (ROWS - row))
                grad_k += trail * dot(vh, near, (1, 1))
                grad_v += trail * dot(kh, near, (1, 0))
            dq_in[:, cols] = grad_q
            dk_in[:, cols] = grad_k
            dv_in[:, cols] = grad_v

        for reads_back in (True, False):

            @pl.when(core == int(reads_back))
            def _():
                one(2 * pair, reads_back)
                one(2 * pair + 1, reads_back)

        return carry

    def finish(heads):
        for head in heads:
            r = rates[head]
            cols = cols_of(head)
            row = row_index() + (core * ROWS).astype(F32)
            lead = jnp.exp(-r * (row + 1.0))
            trail = jnp.exp(-r * (2.0 * ROWS - row))
            before = states[head, :, 0].reshape(DH, DH)
            after = states[head, :, 1].reshape(DH, DH)
            dq[:, cols] = (dq_in[:, cols] + lead * dot(g[:, cols], before, (1, 1))).astype(BF16)
            dk[:, cols] = (dk_in[:, cols] + trail * dot(v[:, cols], after, (1, 1))).astype(BF16)
            dv[:, cols] = (dv_in[:, cols] + trail * dot(k[:, cols], after, (1, 0))).astype(BF16)

    def first_part(t, carry):
        @pl.when(t < CHUNKS)
        def _():
            locals_of(t)

        @pl.when((t >= 1) & (t <= AHEAD))
        def _():
            send_locals(t - 1)

        return carry

    lax.fori_loop(0, CHUNKS + 1, first_part, 0)

    def arrived(c, carry):
        wait_bytes(r_recv.at[c], er.at[c, 1])
        return carry

    lax.fori_loop(0, CHUNKS, arrived, 0)

    def second_part(t, carry):
        @pl.when(t < CHUNKS)
        def _():
            send_plane(t)

        @pl.when(t >= LAG)
        def _():
            send_states(t - LAG)

        lax.fori_loop(jnp.minimum(PAIRS * t, HEADS // 2), jnp.minimum(PAIRS * (t + 1), HEADS // 2), inside, 0)
        return carry

    lax.fori_loop(0, CHUNKS + LAG, second_part, 0)

    def third_part(t, carry):
        @pl.when(t >= 1)
        def _():
            for steps in ((2, 1), (3, 0)):
                heads = []
                for dy in steps:
                    heads.append(set_of(t - 1, 1 - core) + ys_away[dy])
                    wait_bytes(states.at[heads[-1]], xr.at[t - 1, ys_away[dy]])
                finish(heads)

        @pl.when(t < CHUNKS)
        def _():
            for steps in ((2, 1), (3, 0)):
                heads = []
                for dy in steps:
                    owner = ys_away[(YS - dy) % YS]
                    head = set_of(t, core) + owner
                    heads.append(head)
                    came = states.at[head] if dy else states.at[head, pl.ds(0, XS - 1)]
                    wait_bytes(came, sr.at[t, owner])
                    remote(states.at[head], states.at[head], xs.at[t, owner], xr.at[t, owner], sibling).start()
                finish(heads)

        return carry

    lax.fori_loop(0, CHUNKS + 1, third_part, 0)

    def sent(c, carry):
        wait_bytes(r_send.at[c], rs.at[c])
        wait_bytes(r_send.at[c], es.at[c, 0])
        wait_bytes(r_send.at[c], es.at[c, 1])
        wait_bytes(l_recv.at[c, pl.ds(0, CHIPS - 1)], ls.at[c])
        wait_bytes(s_send.at[c, pl.ds(0, CHIPS - 1)], ss.at[c])
        for owner in range(YS):
            wait_bytes(states.at[owner], xs.at[c, owner])
        wait_bytes(z_recv.at[c, pl.ds(0, ZS - 1)], zs.at[c])
        return carry

    lax.fori_loop(0, CHUNKS, sent, 0)


def write_out(dq, dk, dv, dq_hbm, dk_hbm, dv_hbm, sems):
    rows = ROWS // PIECES
    copies = [
        pltpu.make_async_copy(here.at[pl.ds(i * rows, rows)], there.at[pl.ds(i * rows, rows)], sems.at[n, i])
        for n, (here, there) in enumerate(((dq, dq_hbm), (dk, dk_hbm), (dv, dv_hbm)))
        for i in range(PIECES)
    ]
    for copy in copies:
        copy.start()
    for copy in copies:
        copy.wait()


def local(query_rows, key_rows, value_rows, grad_out, decay_rates):
    whole = (ROWS, HEADS * DH)
    sems = pltpu.SemaphoreType.DMA((CHUNKS,))
    owner_sems = pltpu.SemaphoreType.DMA((CHUNKS, SET))
    pair_sems = pltpu.SemaphoreType.DMA((CHUNKS, 2))
    anywhere = pl.BlockSpec(memory_space=pl.ANY)
    grads = pl.pallas_call(
        kernel,
        out_shape=[pltpu.VMEM(whole, BF16)] * 3,
        in_specs=[pl.BlockSpec(memory_space=pltpu.HBM)] + [anywhere] * 4,
        out_specs=[pl.BlockSpec(memory_space=pltpu.VMEM)] * 3,
        scratch_shapes=[pltpu.SMEM((HEADS,), F32), pltpu.SemaphoreType.DMA(())]
        + [pltpu.VMEM(whole, BF16)] * 4
        + [pltpu.VMEM(whole, F32)] * 3
        + [
            pltpu.VMEM((CHUNKS, SET, 2, DH, DH), F32),
            pltpu.VMEM((CHUNKS, SET, DH, DH), BF16),
            pltpu.VMEM((CHUNKS, SET, DH, DH), BF16),
            pltpu.VMEM((HEADS, DH, DH), BF16),
            pltpu.VMEM((HEADS, DH, DH), BF16),
            pltpu.VMEM((CHUNKS, SET, XS, 2, PART, DH), BF16),
            pltpu.VMEM((CHUNKS, CHIPS, 2, PART, DH), BF16),
            pltpu.VMEM((CHUNKS, 2, PART, DH), F32),
            pltpu.VMEM((CHUNKS, ZS, PART, DH), F32),
            pltpu.VMEM((CHUNKS, CHIPS, 2, PART, DH), BF16),
            pltpu.VMEM((HEADS, XS, 2, PART, DH), BF16),
            pltpu.SemaphoreType.DMA((CHUNKS, 4)),
            sems, sems, pair_sems, pair_sems, sems, sems, sems, sems, sems, owner_sems, owner_sems, owner_sems,
        ],
        compiler_params=pltpu.CompilerParams(
            collective_id=0, has_side_effects=True, vmem_limit_bytes=57392 * 1024
        ),
        name="decayed_attention_backward",
    )(decay_rates, query_rows, key_rows, value_rows, grad_out)
    return pl.pallas_call(
        write_out,
        out_shape=[jax.ShapeDtypeStruct(whole, BF16)] * 3,
        in_specs=[anywhere] * 3,
        out_specs=[anywhere] * 3,
        scratch_shapes=[pltpu.SemaphoreType.DMA((3, PIECES))],
        compiler_params=pltpu.CompilerParams(vmem_limit_bytes=1024 * 1024),
        name="write_gradients",
    )(*grads)


def solution(mesh):
    rows = P(("ctx", "head"), None)
    return jax.shard_map(
        local,
        mesh=mesh,
        in_specs=(rows, rows, rows, rows, P()),
        out_specs=(rows, rows, rows),
        check_vma=False,
    )
```
